256 devices in a mesh: rows: 64 (over z_lo, y, x, core), heads: 4 (over z_hi).
Axes of the slice: x: 4, y: 4, z: 8 (z_hi: 4, z_lo: 2; z = z_hi * 2 + z_lo), core: 2. Of those that a mesh axis runs over, the one named last changes fastest.
Arguments:
- signal: bfloat16 [131072, 1024], P('rows'), may hold values from -40 to 40
- w_qkv: bfloat16 [1024, 3072], P(None, 'heads'), may hold values from -1 to 1
- w_out: bfloat16 [1024, 1024], P('heads'), may hold values from -0.1875 to 0.1875
Outputs:
- mixed: bfloat16 [131072, 1024], P('rows', 'heads')
The draws below stay inside these ranges and needn't reach their ends.
All inputs are finite; a program needn't handle non-finite values.
Results may differ from the reference program's by a relative error of at most 0.0082.
Values may be sent and summed in bfloat16 or wider, within the bound.
No kernel may reach another device: no remote copies, remote signals or barrier semaphores. Data moves between devices by JAX's collectives and lax.ppermute only.
A program may use at most 64 MiB of HBM per device.

```python
import jax
import jax.numpy as jnp
from jax import lax

D = 1024
HEADS = 16
C = 512
ROWS = 256
TOKENS = 131072
N_HEADS = 4


def draw_signal(key, part):
    key = jax.random.fold_in(key, 11)
    values_out = jax.random.normal(key, (TOKENS, D), jnp.float32)
    return jnp.clip(values_out, -40.0, 40.0).astype(jnp.bfloat16)


def draw_w_qkv(key, part):
    key = jax.random.fold_in(key, 23)
    scale_factor = 1.0 / jnp.sqrt(jnp.float32(D))
    base = jax.random.normal(key, (D, N_HEADS, 3, D // N_HEADS), jnp.float32) * scale_factor
    bound_value = 6.0 * scale_factor
    return jnp.clip(base, -bound_value, bound_value).reshape(D, 3 * D).astype(jnp.bfloat16)


def block_levels(key, shape, pieces, low, top_value):
    def one(dim, parts):
        heights = jax.random.uniform(jax.random.fold_in(jax.random.fold_in(key, 6), dim), (parts,), jnp.float32, low / len(pieces), top_value / len(pieces))
        return jnp.repeat(jnp.exp(heights), shape[dim] // parts).reshape((-1,) + (1,) * (len(shape) - dim - 1))

    gain = one(*pieces[0])
    for cut in pieces[1:]:
        gain = gain * one(*cut)
    return gain


def centred(rng, extent, deviation, reach, shards=(), held_as=jnp.bfloat16):
    drawn = deviation * jax.random.normal(rng, extent, jnp.float32)
    if shards:
        drawn = drawn * block_levels(rng, extent, shards, -0.22, 0.18)
    return jnp.clip(drawn, -reach, reach).astype(held_as)


def setup_inputs(seed: int = 0) -> dict:
    seeds = jax.random.split(jax.random.key(seed), 4)
    return {
        "signal": draw_signal(jax.random.fold_in(seeds[3], 71), 0),
        "w_qkv": draw_w_qkv(jax.random.fold_in(seeds[3], 71), 0),
        "w_out": centred(seeds[2], (D, D), D ** -0.5, 0.1875, ((0, 4),)),
    }


def attend(queries, keys_in, values_in):
    length = queries.shape[0]
    scale_factor = 1.0 / jnp.sqrt(jnp.float32(queries.shape[-1]))
    scores = jnp.einsum('qhe,khe->hqk', queries.astype(jnp.float32), keys_in.astype(jnp.float32)) * scale_factor
    position = jnp.arange(length, dtype=jnp.int32)
    causal_mask = position[None, :] <= position[:, None]
    scores = jnp.where(causal_mask[None], scores, jnp.float32(-1e+30))
    top_score = lax.optimization_barrier(jnp.max(scores, axis=-1, keepdims=True))
    expo = jnp.exp(scores - top_score)
    weights_bf = (expo / lax.optimization_barrier(jnp.sum(expo, axis=-1, keepdims=True))).astype(jnp.bfloat16)
    result = jnp.einsum('hqk,khe->qhe', weights_bf.astype(jnp.float32), values_in.astype(jnp.float32))
    return result.astype(jnp.bfloat16)

def reference(signal, w_qkv, w_out):
    local_heads = HEADS // N_HEADS
    half_heads = local_heads // 2
    head_dim = D // HEADS
    projected = jnp.dot(signal, w_qkv, preferred_element_type=jnp.float32).astype(jnp.bfloat16)
    projected = projected.reshape(ROWS, C, N_HEADS, 3, local_heads, head_dim)
    row_part = jnp.transpose(projected[:, :, :, :, :half_heads], (0, 1, 3, 2, 4, 5))
    row_part = row_part.reshape(ROWS, C, 3, N_HEADS * half_heads, head_dim)

    def row_block(block):
        return attend(block[:, 0], block[:, 1], block[:, 2])
    row_out = lax.map(row_block, row_part)
    col_part = jnp.transpose(projected[:, :, :, :, half_heads:], (1, 0, 3, 2, 4, 5))
    col_part = col_part.reshape(C, ROWS, 3, N_HEADS * half_heads, head_dim)
    col_out = lax.map(row_block, col_part)
    col_out = jnp.transpose(col_out, (1, 0, 2, 3))
    row_out = row_out.reshape(ROWS, C, N_HEADS, half_heads, head_dim)
    col_out = col_out.reshape(ROWS, C, N_HEADS, half_heads, head_dim)
    attended = jnp.concatenate([row_out, col_out], axis=3).reshape(TOKENS, D)
    return jnp.dot(attended, w_out, preferred_element_type=jnp.float32).astype(jnp.bfloat16)
```

```python
import jax
import jax.numpy as jnp
from jax import lax
from jax.experimental import pallas as pl
from jax.experimental.pallas import tpu as pltpu
from jax.sharding import PartitionSpec as P

D = 1024
HEADS = 16
C = 512
GROUPS = 4
DIM = 64
HALF = 128
ROWS_LOCAL = 4
BLOCK = 128
BF = jnp.bfloat16
F32 = jnp.float32
VMEM = pltpu.VMEM
MIB = 1 << 20


def whole():
    return pl.BlockSpec(memory_space=VMEM)


def anywhere():
    return pl.BlockSpec(memory_space=pl.ANY)


def smem():
    return pl.BlockSpec(memory_space=pltpu.SMEM)


def one_hot(source_of):
    out_at = lax.broadcasted_iota(jnp.int32, (BLOCK, BLOCK), 0)
    in_at = lax.broadcasted_iota(jnp.int32, (BLOCK, BLOCK), 1)
    return (in_at == source_of(out_at)).astype(F32).astype(BF)


def move(pick, data):
    return jnp.dot(pick, data, preferred_element_type=F32).astype(BF)


def attend(qkv, length, store):
    lane = lax.broadcasted_iota(jnp.int32, (1, HALF), 1)
    first = lane < DIM
    query = qkv[:, :HALF]
    query_a = jnp.where(first, query, 0.0).astype(BF)
    query_b = jnp.where(first, 0.0, query).astype(BF)
    key = qkv[:, HALF : 2 * HALF].astype(BF)
    value = qkv[:, 2 * HALF :].astype(BF)
    for block in range(length // BLOCK):
        lo = block * BLOCK
        hi = lo + BLOCK
        both = jnp.concatenate([query_a[lo:hi], query_b[lo:hi]], axis=0)
        scores = lax.dot_general(
            both, key[:hi], (((1,), (1,)), ((), ())), preferred_element_type=F32
        )
        at_query = lax.broadcasted_iota(jnp.int32, scores.shape, 0) % BLOCK + lo
        at_key = lax.broadcasted_iota(jnp.int32, scores.shape, 1)
        scores = jnp.where(at_key <= at_query, scores, F32(-1e30))
        top = jnp.max(scores, axis=-1, keepdims=True)
        expo = jnp.exp((scores - top) * F32(0.125))
        total = jnp.sum(expo, axis=-1, keepdims=True)
        out = jnp.dot(expo.astype(BF), value[:hi], preferred_element_type=F32) / total
        store(block, jnp.where(first, out[:BLOCK], out[BLOCK:]).astype(BF))


def prep_kernel(meta, sig_ref, out_ref):
    pick = one_hot(lambda o: ((o // 2) % 4) * 32 + (o // 8) * 2 + o % 2)
    out_ref[...] = move(pick, sig_ref[...].reshape(BLOCK, D))


def prep(meta, sig):
    return pl.pallas_call(
        prep_kernel,
        grid_spec=pltpu.PrefetchScalarGridSpec(
            num_scalar_prefetch=1,
            grid=(4,),
            in_specs=[pl.BlockSpec((4, 32, D), lambda b, meta: (0, meta[0] * 4 + b, 0))],
            out_specs=pl.BlockSpec((BLOCK, D), lambda b, meta: (b, 0)),
        ),
        out_shape=jax.ShapeDtypeStruct((C, D), BF),
        cost_estimate=pl.CostEstimate(flops=2 * C * D * BLOCK, bytes_accessed=2 * MIB, transcendentals=0),
        name="prep",
    )(meta, sig)


def row_kernel(meta, sig_ref, w_ref, out0, out1, out2, out3, held):
    g = meta[0]
    weight = jnp.concatenate(
        [w_ref[:, 0:HALF], w_ref[:, 256 : 256 + HALF], w_ref[:, 512 : 512 + HALF]], axis=1
    )
    qkv = jnp.dot(sig_ref[0], weight, preferred_element_type=F32)

    def store(block, out):
        held[block * BLOCK : (block + 1) * BLOCK, :] = out

    attend(qkv, C, store)
    for k, out in enumerate((out0, out1, out2, out3)):
        at = pl.multiple_of(lax.rem(g + k, GROUPS) * BLOCK, BLOCK)
        out[0] = held[pl.ds(at, BLOCK), :]


def row_part(meta, sig, w_qkv):
    return pl.pallas_call(
        row_kernel,
        grid_spec=pltpu.PrefetchScalarGridSpec(
            num_scalar_prefetch=1,
            grid=(ROWS_LOCAL,),
            in_specs=[
                pl.BlockSpec((1, C, D), lambda r, meta: (r, 0, 0)),
                pl.BlockSpec((D, 768), lambda r, meta: (0, 0)),
            ],
            out_specs=[pl.BlockSpec((1, BLOCK, HALF), lambda r, meta: (r, 0, 0))] * GROUPS,
            scratch_shapes=[VMEM((C, HALF), BF)],
        ),
        out_shape=[jax.ShapeDtypeStruct((ROWS_LOCAL, BLOCK, HALF), BF)] * GROUPS,
        compiler_params=pltpu.CompilerParams(vmem_limit_bytes=24 * MIB),
        cost_estimate=pl.CostEstimate(
            flops=6 * 10**9, bytes_accessed=6 * MIB, transcendentals=2 * 10**6
        ),
        name="row_part",
    )(meta, sig, w_qkv)


def column_kernel(meta, got_ref, w_ref, *refs):
    near = refs[0:4]
    far = refs[4:8]
    out_ref, held, weights, outs, sems = refs[8:]
    x = meta[1]
    core = meta[2]
    copies = []
    for d in range(4):
        from_x = lax.rem(x + 4 - d, 4) * 2
        for n, (ref, at) in enumerate(((near[d], from_x + core), (far[d], from_x + 1 - core))):
            rows = pl.ds(pl.multiple_of(at * BLOCK, BLOCK), BLOCK)
            copy = pltpu.make_async_copy(ref, weights.at[:, rows, :], sems.at[2 * d + n])
            copy.start()
            copies.append(copy)
    pick = one_hot(lambda o: (o % 64) * 2 + o // 64)
    for b in range(4):
        moved = move(pick, got_ref[b * BLOCK : (b + 1) * BLOCK, :])
        held[b * 64 : b * 64 + 64, :] = moved[:64]
        held[256 + b * 64 : 256 + b * 64 + 64, :] = moved[64:]

    def group(k, weight):
        qkv = jnp.dot(held[...], weight, preferred_element_type=F32)
        for c in range(2):

            def store(block, out):
                lo = c * 256 + block * BLOCK
                outs[lo : lo + BLOCK, k * HALF : (k + 1) * HALF] = out

            attend(qkv[c * 256 : (c + 1) * 256], 256, store)

    group(
        0,
        jnp.concatenate(
            [w_ref[:, HALF:256], w_ref[:, 256 + HALF : 512], w_ref[:, 512 + HALF :]], axis=1
        ),
    )
    for copy in copies:
        copy.wait()
    for k in range(1, GROUPS):
        group(k, weights[k - 1])
    back = one_hot(lambda o: (o % 2) * 64 + o // 2)
    for b in range(4):
        both = jnp.concatenate(
            [outs[b * 64 : b * 64 + 64, :], outs[256 + b * 64 : 256 + b * 64 + 64, :]], axis=0
        )
        out_ref[b * BLOCK : (b + 1) * BLOCK, :] = move(back, both)


def column_part(meta, got, w_qkv, near, far):
    return pl.pallas_call(
        column_kernel,
        in_specs=[smem(), whole(), whole()] + [anywhere()] * 8,
        out_specs=whole(),
        out_shape=jax.ShapeDtypeStruct((C, C), BF),
        scratch_shapes=[
            VMEM((C, D), BF),
            VMEM((3, D, 3 * HALF), BF),
            VMEM((C, C), BF),
            pltpu.SemaphoreType.DMA((8,)),
        ],
        compiler_params=pltpu.CompilerParams(vmem_limit_bytes=24 * MIB),
        cost_estimate=pl.CostEstimate(
            flops=4 * 10**9, bytes_accessed=6 * MIB, transcendentals=10**6
        ),
        name="column_part",
    )(meta, got, w_qkv, *near, *far)


def out_kernel(meta, got_ref, row0, row1, row2, row3, *refs):
    own = refs[0]
    near = refs[1:4]
    far = refs[4:7]
    outs = refs[7:11]
    weights, attended, sems = refs[11:]
    g = meta[0]
    core = meta[2]
    copies = [pltpu.make_async_copy(own, weights.at[pl.ds(0, 256), :], sems.at[0])]
    for k in range(1, GROUPS):
        for n, (ref, at) in enumerate(((near[k - 1], core), (far[k - 1], 1 - core))):
            rows = pl.ds(pl.multiple_of(k * 256 + at * BLOCK, BLOCK), BLOCK)
            copies.append(
                pltpu.make_async_copy(ref, weights.at[rows, :], sems.at[2 * k - 1 + n])
            )
    for copy in copies:
        copy.start()
    for k, row in enumerate((row0, row1, row2, row3)):
        attended[:, k * 256 : k * 256 + HALF] = row[...].reshape(C, HALF)
    pick = one_hot(lambda o: ((o // 2) % 16) * 8 + (o // 32) * 2 + o % 2)
    for b in range(4):
        moved = move(pick, got_ref[b * BLOCK : (b + 1) * BLOCK, :])
        for r in range(ROWS_LOCAL):
            lo = r * BLOCK + b * 32
            for k in range(GROUPS):
                attended[lo : lo + 32, k * 256 + HALF : (k + 1) * 256] = moved[
                    r * 32 : (r + 1) * 32, k * HALF : (k + 1) * HALF
                ]
    for copy in copies:
        copy.wait()
    left = attended[...]
    for k in range(GROUPS):
        at = pl.multiple_of(lax.rem(g + k, GROUPS) * 256, 256)
        outs[k][...] = jnp.dot(
            left, weights[:, pl.ds(at, 256)], preferred_element_type=F32
        ).astype(BF)


def out_part(meta, got, rows, own, near, far):
    return pl.pallas_call(
        out_kernel,
        in_specs=[smem()] + [whole()] * 5 + [anywhere()] * 7,
        out_specs=[whole()] * GROUPS,
        out_shape=[jax.ShapeDtypeStruct((C, 256), BF)] * GROUPS,
        scratch_shapes=[
            VMEM((D, D), BF),
            VMEM((C, D), BF),
            pltpu.SemaphoreType.DMA((7,)),
        ],
        compiler_params=pltpu.CompilerParams(vmem_limit_bytes=24 * MIB),
        cost_estimate=pl.CostEstimate(
            flops=10**9, bytes_accessed=5 * MIB, transcendentals=0
        ),
        name="out_part",
    )(meta, got, *rows, own, *near, *far)


def place_kernel(meta, in0, in1, in2, in3, out_ref, sems):
    g = meta[0]
    copies = []
    for k, ref in enumerate((in0, in1, in2, in3)):
        at = lax.rem(g + GROUPS - k, GROUPS)
        copies.append(pltpu.make_async_copy(ref, out_ref.at[:, at], sems.at[k]))
    for copy in copies:
        copy.start()
    for copy in copies:
        copy.wait()


def place(meta, parts):
    return pl.pallas_call(
        place_kernel,
        in_specs=[smem()] + [anywhere()] * GROUPS,
        out_specs=anywhere(),
        out_shape=jax.ShapeDtypeStruct((ROWS_LOCAL, GROUPS, BLOCK, 256), BF),
        scratch_shapes=[pltpu.SemaphoreType.DMA((GROUPS,))],
        cost_estimate=pl.CostEstimate(flops=0, bytes_accessed=2 * MIB, transcendentals=0),
        name="place",
    )(meta, *[part.reshape(ROWS_LOCAL, BLOCK, 256) for part in parts])


def to_group(data, k):
    return lax.ppermute(data, "heads", [(j, (j + k) % GROUPS) for j in range(GROUPS)])


def along_x(data, d):
    return lax.ppermute(
        data, "rows", [(i, i // 8 * 8 + (i // 2 % 4 + d) % 4 * 2 + i % 2) for i in range(64)]
    )


def other_core(data):
    return lax.ppermute(data, "rows", [(i, i ^ 1) for i in range(64)])


def local(signal, w_qkv, w_out):
    i = lax.axis_index("rows")
    g = lax.axis_index("heads")
    core = i % 2
    x = i // 2 % 4
    meta = jnp.stack([g, x, core]).astype(jnp.int32)
    sig = signal.reshape(ROWS_LOCAL, C, D)

    mine = lax.dynamic_slice_in_dim(w_qkv, (i % 8) * BLOCK, BLOCK, axis=0)
    mine = jnp.concatenate([mine[:, HALF:256], mine[:, 256 + HALF : 512], mine[:, 512 + HALF :]], axis=1)
    others = jnp.stack([to_group(mine, k) for k in (1, 2, 3)])
    near = [others] + [along_x(others, d) for d in (1, 2, 3)]
    far = [other_core(part) for part in near]

    send = prep(meta, sig).reshape(64, 8, D)
    got = lax.all_to_all(send, "rows", split_axis=0, concat_axis=0, tiled=True).reshape(C, D)

    rows = row_part(meta, sig, w_qkv)
    rows = [rows[0]] + [to_group(rows[k], k) for k in (1, 2, 3)]

    half = lax.dynamic_slice_in_dim(w_out, core * BLOCK, BLOCK, axis=0)
    out_near = [to_group(half, k) for k in (1, 2, 3)]
    out_far = [other_core(part) for part in out_near]

    columns = column_part(meta, got, w_qkv, near, far).reshape(64, 8, C)
    back = lax.all_to_all(columns, "rows", split_axis=0, concat_axis=0, tiled=True).reshape(C, C)

    parts = out_part(meta, back, rows, w_out, out_near, out_far)
    parts = [parts[0]] + [to_group(parts[k], k) for k in (1, 2, 3)]
    return place(meta, parts).reshape(ROWS_LOCAL * C, 256)


def solution(mesh):
    return jax.shard_map(
        local,
        mesh=mesh,
        in_specs=(P("rows", None), P(None, "heads"), P("heads", None)),
        out_specs=P("rows", "heads"),
        check_vma=False,
    )
```

```python
import jax
import jax.numpy as jnp
from jax import lax
from jax.experimental import pallas as pl
from jax.experimental.pallas import tpu as pltpu
from jax.sharding import PartitionSpec as P

D = 1024
HEADS = 16
C = 512
GROUPS = 4
DIM = 64
HALF = 128
ROWS_LOCAL = 4
BLOCK = 128
BF = jnp.bfloat16
F32 = jnp.float32
VMEM = pltpu.VMEM
MIB = 1 << 20
ORDER = (2, 1, 3)
SCALE = 0.125 * 1.4426950408889634


def whole():
    return pl.BlockSpec(memory_space=VMEM)


def anywhere():
    return pl.BlockSpec(memory_space=pl.ANY)


def smem():
    return pl.BlockSpec(memory_space=pltpu.SMEM)


def one_hot(source_of):
    out_at = lax.broadcasted_iota(jnp.int32, (BLOCK, BLOCK), 0)
    in_at = lax.broadcasted_iota(jnp.int32, (BLOCK, BLOCK), 1)
    return (in_at == source_of(out_at)).astype(F32).astype(BF)


def move(pick, data):
    return jnp.dot(pick, data, preferred_element_type=F32).astype(BF)


def causal():
    at_query = lax.broadcasted_iota(jnp.int32, (2 * BLOCK, BLOCK), 0) % BLOCK
    return lax.broadcasted_iota(jnp.int32, (2 * BLOCK, BLOCK), 1) <= at_query


def attend(qkv, allowed, store):
    length = qkv.shape[0]
    first = lax.broadcasted_iota(jnp.int32, (1, HALF), 1) < DIM
    query = qkv[:, :HALF]
    query_a = jnp.where(first, query, 0.0).astype(BF)
    query_b = jnp.where(first, 0.0, query).astype(BF)
    key = qkv[:, HALF : 2 * HALF].astype(BF)
    value = qkv[:, 2 * HALF :].astype(BF)
    value = jnp.concatenate([value, jnp.ones((length, HALF), BF)], axis=1)
    for block in range(length // BLOCK):
        lo = block * BLOCK
        hi = lo + BLOCK
        both = jnp.concatenate([query_a[lo:hi], query_b[lo:hi]], axis=0)
        scores = lax.dot_general(
            both, key[:hi], (((1,), (1,)), ((), ())), preferred_element_type=F32
        )
        pieces = [scores[:, n * BLOCK : (n + 1) * BLOCK] for n in range(block)]
        pieces.append(jnp.where(allowed, scores[:, lo:], F32(-1e30)))
        top = pieces[0]
        for piece in pieces[1:]:
            top = jnp.maximum(top, piece)
        top = jnp.max(top, axis=-1, keepdims=True)
        expo = [jnp.exp2((piece - top) * F32(SCALE)).astype(BF) for piece in pieces]
        out = jnp.dot(jnp.concatenate(expo, axis=1), value[:hi], preferred_element_type=F32)
        out = jnp.where(jnp.concatenate([first, first], axis=1), out[:BLOCK], out[BLOCK:])
        store(lo, (out[:, :HALF] / out[:, HALF:]).astype(BF))


def call(kernel, name, flops=0, moved=MIB, **options):
    return pl.pallas_call(
        kernel,
        compiler_params=pltpu.CompilerParams(vmem_limit_bytes=56 * MIB),
        cost_estimate=pl.CostEstimate(flops=flops, bytes_accessed=moved, transcendentals=0),
        name=name,
        **options,
    )


def like(*shape):
    return jax.ShapeDtypeStruct(shape, BF)


def cut_kernel(meta, query_ref, key_ref, value_ref, col_ref, row_ref, *outs):
    g = meta[0]
    for k, out_ref in zip(ORDER, outs):
        out_ref[:, :HALF] = query_ref[...]
        out_ref[:, HALF : 2 * HALF] = key_ref[...]
        out_ref[:, 2 * HALF : 3 * HALF] = value_ref[...]
        out_ref[:, 3 * HALF : 4 * HALF] = col_ref[...]
        at = pl.multiple_of(lax.rem(g + k, GROUPS) * 256, 256)
        out_ref[:, 4 * HALF :] = row_ref[:, pl.ds(at, 256)]


def cut(meta, w_qkv, w_out):
    def part(n):
        return pl.BlockSpec((BLOCK, HALF), lambda b, meta: (meta[1] * 2 + meta[2], 2 * n + 1))

    return call(
        cut_kernel,
        "cut",
        grid_spec=pltpu.PrefetchScalarGridSpec(
            num_scalar_prefetch=1,
            grid=(1,),
            in_specs=[
                part(0),
                part(1),
                part(2),
                pl.BlockSpec((BLOCK, HALF), lambda b, meta: (1, meta[1] * 2 + meta[2])),
                pl.BlockSpec((BLOCK, D), lambda b, meta: (0, 0)),
            ],
            out_specs=[pl.BlockSpec((BLOCK, 6 * HALF), lambda b, meta: (0, 0))] * 3,
        ),
        out_shape=[like(BLOCK, 6 * HALF)] * 3,
    )(meta, w_qkv, w_qkv, w_qkv, w_out, w_out)


def mid_kernel(in0, in1, in2, out_ref, row_ref):
    for n, ref in enumerate((in0, in1, in2)):
        out_ref[n] = ref[:, : 4 * HALF]
        row_ref[n] = ref[:, 4 * HALF :]


def mid(parts):
    return call(
        mid_kernel,
        "mid",
        flops=10**12,
        in_specs=[whole()] * 3,
        out_specs=[whole()] * 2,
        out_shape=[like(3, BLOCK, 4 * HALF), like(3, BLOCK, 256)],
    )(*parts)


def stack_kernel(in0, in1, in2, in3, after, out_ref):
    for n, ref in enumerate((in0, in1, in2, in3)):
        out_ref[n] = ref[...]


def stack(parts, after):
    return call(
        stack_kernel,
        "stack",
        flops=10**9,
        in_specs=[whole()] * 4 + [anywhere()],
        out_specs=whole(),
        out_shape=like(4, 3, BLOCK, 4 * HALF),
    )(*parts, after)


def prep_kernel(meta, sig_ref, out_ref):
    pick = one_hot(lambda o: ((o // 2) % 4) * 32 + (o // 8) * 2 + o % 2)
    for b in range(2):
        part = sig_ref[:, b * 32 : (b + 1) * 32, :].reshape(BLOCK, D)
        out_ref[b * BLOCK : (b + 1) * BLOCK, :] = move(pick, part)


def prep(meta, sig):
    return call(
        prep_kernel,
        "prep",
        flops=2 * C * D * BLOCK,
        moved=2 * MIB,
        grid_spec=pltpu.PrefetchScalarGridSpec(
            num_scalar_prefetch=1,
            grid=(2,),
            in_specs=[pl.BlockSpec((4, 64, D), lambda b, meta: (0, meta[0] * 2 + b, 0))],
            out_specs=pl.BlockSpec((256, D), lambda b, meta: (b, 0)),
        ),
        out_shape=like(C, D),
    )(meta, sig)


def row_kernel(sig_ref, query_ref, key_ref, value_ref, out_ref):
    weight = jnp.concatenate([query_ref[...], key_ref[...], value_ref[...]], axis=1)
    qkv = jnp.dot(sig_ref[0], weight, preferred_element_type=F32)

    def store(lo, out):
        out_ref[0, lo : lo + BLOCK, :] = out

    attend(qkv, causal(), store)


def row_part(sig, w_qkv):
    def part(n):
        return pl.BlockSpec((D, HALF), lambda r: (0, 2 * n))

    return call(
        row_kernel,
        "row_part",
        flops=6 * 10**9,
        moved=6 * MIB,
        grid=(ROWS_LOCAL,),
        in_specs=[pl.BlockSpec((1, C, D), lambda r: (r, 0, 0)), part(0), part(1), part(2)],
        out_specs=pl.BlockSpec((1, C, HALF), lambda r: (r, 0, 0)),
        out_shape=like(ROWS_LOCAL, C, HALF),
    )(sig, w_qkv, w_qkv, w_qkv)


def column_kernel(
    meta, got_ref, w_ref, w_out_ref, near, far, out_ref, held, weights, mixers, outs, sems
):
    x = meta[1]
    core = meta[2]
    copies = []
    for d in range(4):
        from_x = lax.rem(x + 4 - d, 4) * 2
        for n, (ref, at) in enumerate(((near, from_x + core), (far, from_x + 1 - core))):
            rows = pl.ds(pl.multiple_of(at * BLOCK, BLOCK), BLOCK)
            sem = 4 * d + 2 * n
            copies.append(
                pltpu.make_async_copy(
                    ref.at[d, :, :, : 3 * HALF], weights.at[:, rows, :], sems.at[sem]
                )
            )
            copies.append(
                pltpu.make_async_copy(
                    ref.at[d, :, :, 3 * HALF :], mixers.at[:, at], sems.at[sem + 1]
                )
            )
    for copy in copies:
        copy.start()
    pick = one_hot(lambda o: (o % 64) * 2 + o // 64)
    for b in range(4):
        moved = move(pick, got_ref[b * BLOCK : (b + 1) * BLOCK, :])
        held[b * 64 : b * 64 + 64, :] = moved[:64]
        held[256 + b * 64 : 256 + b * 64 + 64, :] = moved[64:]
    allowed = causal()

    def group(k, weight):
        qkv = jnp.dot(held[...], weight, preferred_element_type=F32)
        for c in range(2):

            def store(lo, out):
                at = c * 256 + lo
                outs[at : at + BLOCK, k * HALF : (k + 1) * HALF] = out

            attend(qkv[c * 256 : (c + 1) * 256], allowed, store)

    group(
        0,
        jnp.concatenate(
            [w_ref[:, HALF:256], w_ref[:, 256 + HALF : 512], w_ref[:, 512 + HALF :]], axis=1
        ),
    )
    for copy in copies:
        copy.wait()
    for n in range(3):
        group(n + 1, weights[n])
    mixer = jnp.concatenate(
        [w_out_ref[HALF:, :]]
        + [jnp.concatenate([mixers[n, s] for s in range(8)], axis=1) for n in range(3)],
        axis=0,
    )
    back = one_hot(lambda o: (o % 2) * 64 + o // 2)
    for b in range(4):
        both = jnp.concatenate(
            [outs[b * 64 : b * 64 + 64, :], outs[256 + b * 64 : 256 + b * 64 + 64, :]], axis=0
        )
        mixed = jnp.dot(move(back, both), mixer, preferred_element_type=F32).astype(BF)
        for j in range(GROUPS):
            out_ref[b * 16 : (b + 1) * 16, j] = mixed[:, j * 256 : (j + 1) * 256].reshape(16, 8, 256)


def column_part(meta, got, w_qkv, w_out, near, far):
    return call(
        column_kernel,
        "column_part",
        flops=4 * 10**9,
        moved=6 * MIB,
        in_specs=[smem(), whole(), whole(), whole(), anywhere(), anywhere()],
        out_specs=whole(),
        out_shape=like(64, GROUPS, 8, 256),
        scratch_shapes=[
            VMEM((C, D), BF),
            VMEM((3, D, 3 * HALF), BF),
            VMEM((3, 8, BLOCK, HALF), BF),
            VMEM((C, C), BF),
            pltpu.SemaphoreType.DMA((16,)),
        ],
    )(meta, got, w_qkv, w_out, near, far)


def join_kernel(meta, got_ref, rows_ref, own_ref, w_ref, out_ref):
    g = meta[0]
    weight = jnp.concatenate([own_ref[...]] + [w_ref[n] for n in range(3)], axis=0)
    pick = one_hot(lambda o: ((o // 2) % 16) * 8 + (o // 32) * 2 + o % 2)
    columns = [
        jnp.dot(
            pick,
            got_ref[b * 16 : (b + 1) * 16, 0].reshape(BLOCK, 256),
            preferred_element_type=F32,
        )
        for b in range(4)
    ]
    for r in range(ROWS_LOCAL):
        left = jnp.concatenate(
            [rows_ref[lax.rem(g + GROUPS - k, GROUPS), r, 0] for k in (0,) + ORDER], axis=1
        )
        right = jnp.concatenate([column[r * 32 : (r + 1) * 32] for column in columns], axis=0)
        mixed = jnp.dot(left, weight, preferred_element_type=F32) + right
        out_ref[r, 0] = mixed.astype(BF)


def join(meta, got, rows, w_out, w_rows):
    return call(
        join_kernel,
        "join",
        flops=2 * 10**9,
        moved=4 * MIB,
        grid_spec=pltpu.PrefetchScalarGridSpec(
            num_scalar_prefetch=1,
            grid=(GROUPS,),
            in_specs=[
                pl.BlockSpec((64, 1, 8, 256), lambda j, meta: (0, j, 0, 0)),
                pl.BlockSpec(
                    (GROUPS, ROWS_LOCAL, 1, BLOCK, HALF), lambda j, meta: (0, 0, j, 0, 0)
                ),
                pl.BlockSpec((BLOCK, 256), lambda j, meta: (0, meta[0])),
                pl.BlockSpec((3, BLOCK, 256), lambda j, meta: (0, 0, 0)),
            ],
            out_specs=pl.BlockSpec((ROWS_LOCAL, 1, BLOCK, 256), lambda j, meta: (0, j, 0, 0)),
        ),
        out_shape=like(ROWS_LOCAL, GROUPS, BLOCK, 256),
    )(meta, got, rows, w_out, w_rows)


def to_group(data, k):
    return lax.ppermute(data, "heads", [(j, (j + k) % GROUPS) for j in range(GROUPS)])


def along_x(data, d):
    return lax.ppermute(
        data, "rows", [(i, i // 8 * 8 + (i // 2 % 4 + d) % 4 * 2 + i % 2) for i in range(64)]
    )


def other_core(data):
    return lax.ppermute(data, "rows", [(i, i ^ 1) for i in range(64)])


def local(signal, w_qkv, w_out):
    i = lax.axis_index("rows")
    g = lax.axis_index("heads")
    meta = jnp.stack([g, i // 2 % 4, i % 2]).astype(jnp.int32)
    sig = signal.reshape(ROWS_LOCAL, C, D)

    cuts = cut(meta, w_qkv, w_out)
    others, w_rows = mid([to_group(part, k) for part, k in zip(cuts, ORDER)])

    send = prep(meta, sig).reshape(64, 8, D)
    got = lax.all_to_all(send, "rows", split_axis=0, concat_axis=0, tiled=True).reshape(C, D)

    own_rows = row_part(sig, w_qkv)
    rows = lax.all_gather(own_rows.reshape(ROWS_LOCAL * C, HALF), "heads", axis=0)

    near = stack([others] + [along_x(others, d) for d in (1, 2, 3)], own_rows)
    far = other_core(near)

    columns = column_part(meta, got, w_qkv, w_out, near, far).reshape(64 * GROUPS, 8, 256)
    back = lax.all_to_all(columns, ("rows", "heads"), split_axis=0, concat_axis=0, tiled=True)
    return join(
        meta,
        back.reshape(64, GROUPS, 8, 256),
        rows.reshape(GROUPS, ROWS_LOCAL, GROUPS, BLOCK, HALF),
        w_out,
        w_rows,
    ).reshape(ROWS_LOCAL * C, 256)


def solution(mesh):
    return jax.shard_map(
        local,
        mesh=mesh,
        in_specs=(P("rows", None), P(None, "heads"), P("heads", None)),
        out_specs=P("rows", "heads"),
        check_vma=False,
    )
```

```python
import jax
import jax.numpy as jnp
from jax import lax
from jax.experimental import pallas as pl
from jax.experimental.pallas import tpu as pltpu
from jax.sharding import PartitionSpec as P

D = 1024
HEADS = 16
C = 512
GROUPS = 4
DIM = 64
HALF = 128
ROWS_LOCAL = 4
BLOCK = 128
BF = jnp.bfloat16
F32 = jnp.float32
VMEM = pltpu.VMEM
MIB = 1 << 20
ORDER = (2, 1, 3)
SCALE = 0.125 * 1.4426950408889634


def whole():
    return pl.BlockSpec(memory_space=VMEM)


def anywhere():
    return pl.BlockSpec(memory_space=pl.ANY)


def smem():
    return pl.BlockSpec(memory_space=pltpu.SMEM)


def one_hot(source_of):
    out_at = lax.broadcasted_iota(jnp.int32, (BLOCK, BLOCK), 0)
    in_at = lax.broadcasted_iota(jnp.int32, (BLOCK, BLOCK), 1)
    return (in_at == source_of(out_at)).astype(F32).astype(BF)


def move(pick, data):
    return jnp.dot(pick, data, preferred_element_type=F32).astype(BF)


def causal():
    at_query = lax.broadcasted_iota(jnp.int32, (2 * BLOCK, BLOCK), 0) % BLOCK
    return lax.broadcasted_iota(jnp.int32, (2 * BLOCK, BLOCK), 1) <= at_query


def attend(qkv, allowed, store):
    length = qkv.shape[0]
    first = lax.broadcasted_iota(jnp.int32, (1, HALF), 1) < DIM
    query = qkv[:, :HALF]
    query_a = jnp.where(first, query, 0.0).astype(BF)
    query_b = jnp.where(first, 0.0, query).astype(BF)
    key = qkv[:, HALF : 2 * HALF].astype(BF)
    value = qkv[:, 2 * HALF :].astype(BF)
    value = jnp.concatenate([value, jnp.ones((length, HALF), BF)], axis=1)
    for block in range(length // BLOCK):
        lo = block * BLOCK
        hi = lo + BLOCK
        both = jnp.concatenate([query_a[lo:hi], query_b[lo:hi]], axis=0)
        scores = lax.dot_general(
            both, key[:hi], (((1,), (1,)), ((), ())), preferred_element_type=F32
        )
        pieces = [scores[:, n * BLOCK : (n + 1) * BLOCK] for n in range(block)]
        pieces.append(jnp.where(allowed, scores[:, lo:], F32(-1e30)))
        top = pieces[0]
        for piece in pieces[1:]:
            top = jnp.maximum(top, piece)
        top = jnp.max(top, axis=-1, keepdims=True)
        expo = [jnp.exp2((piece - top) * F32(SCALE)).astype(BF) for piece in pieces]
        out = jnp.dot(jnp.concatenate(expo, axis=1), value[:hi], preferred_element_type=F32)
        out = jnp.where(jnp.concatenate([first, first], axis=1), out[:BLOCK], out[BLOCK:])
        store(lo, (out[:, :HALF] / out[:, HALF:]).astype(BF))


def call(kernel, name, flops=0, moved=MIB, **options):
    return pl.pallas_call(
        kernel,
        compiler_params=pltpu.CompilerParams(vmem_limit_bytes=56 * MIB),
        cost_estimate=pl.CostEstimate(flops=flops, bytes_accessed=moved, transcendentals=0),
        name=name,
        **options,
    )


def like(*shape):
    return jax.ShapeDtypeStruct(shape, BF)


def cut_kernel(meta, query_ref, key_ref, value_ref, col_ref, row_ref, out_ref, *rows):
    g = meta[0]
    out_ref[:, :HALF] = query_ref[...]
    out_ref[:, HALF : 2 * HALF] = key_ref[...]
    out_ref[:, 2 * HALF : 3 * HALF] = value_ref[...]
    out_ref[:, 3 * HALF :] = col_ref[...]
    for k, ref in zip(ORDER, rows):
        at = pl.multiple_of(lax.rem(g + k, GROUPS) * 256, 256)
        ref[...] = row_ref[:, pl.ds(at, 256)]


def cut(meta, w_qkv, w_out):
    def part(n, axis):
        return pl.BlockSpec((BLOCK, HALF), lambda b, meta: (meta[axis] * 2 + meta[2], 2 * n + 1))

    return call(
        cut_kernel,
        "cut",
        grid_spec=pltpu.PrefetchScalarGridSpec(
            num_scalar_prefetch=1,
            grid=(1,),
            in_specs=[
                part(0, 1),
                part(1, 1),
                part(2, 3),
                pl.BlockSpec((BLOCK, HALF), lambda b, meta: (1, meta[3] * 2 + meta[2])),
                pl.BlockSpec((BLOCK, D), lambda b, meta: (0, 0)),
            ],
            out_specs=[pl.BlockSpec((BLOCK, 4 * HALF), lambda b, meta: (0, 0))]
            + [pl.BlockSpec((BLOCK, 256), lambda b, meta: (0, 0))] * 3,
        ),
        out_shape=[like(BLOCK, 4 * HALF)] + [like(BLOCK, 256)] * 3,
    )(meta, w_qkv, w_qkv, w_qkv, w_out, w_out)


def mid_kernel(in0, in1, in2, x_ref, y_ref):
    for n, ref in enumerate((in0, in1, in2)):
        x_ref[n] = ref[:, :256]
        y_ref[n] = ref[:, 256:]


def mid(parts):
    return call(
        mid_kernel,
        "mid",
        flops=10**12,
        in_specs=[whole()] * 3,
        out_specs=[whole()] * 2,
        out_shape=[like(3, BLOCK, 256)] * 2,
    )(*parts)


def stack_kernel(*refs):
    out_ref = refs[-1]
    for n in range(8):
        out_ref[n // 4, n % 4] = refs[n][...]


def stack(parts, after):
    return call(
        stack_kernel,
        "stack",
        flops=10**9,
        in_specs=[whole()] * 8 + [anywhere()] * len(after),
        out_specs=whole(),
        out_shape=like(2, 4, 3, BLOCK, 256),
    )(*parts, *after)


def prep_kernel(meta, sig_ref, out_ref):
    pick = one_hot(lambda o: ((o // 2) % 4) * 32 + (o // 8) * 2 + o % 2)
    for b in range(2):
        part = sig_ref[:, b * 32 : (b + 1) * 32, :].reshape(BLOCK, D)
        out_ref[b * BLOCK : (b + 1) * BLOCK, :] = move(pick, part)


def prep(meta, sig):
    return call(
        prep_kernel,
        "prep",
        flops=2 * C * D * BLOCK,
        moved=2 * MIB,
        grid_spec=pltpu.PrefetchScalarGridSpec(
            num_scalar_prefetch=1,
            grid=(2,),
            in_specs=[pl.BlockSpec((4, 64, D), lambda b, meta: (0, meta[0] * 2 + b, 0))],
            out_specs=pl.BlockSpec((256, D), lambda b, meta: (b, 0)),
        ),
        out_shape=like(C, D),
    )(meta, sig)


def row_kernel(sig_ref, query_ref, key_ref, value_ref, out_ref):
    weight = jnp.concatenate([query_ref[...], key_ref[...], value_ref[...]], axis=1)
    qkv = jnp.dot(sig_ref[0], weight, preferred_element_type=F32)

    def store(lo, out):
        out_ref[0, lo : lo + BLOCK, :] = out

    attend(qkv, causal(), store)


def row_part(sig, w_qkv):
    def part(n):
        return pl.BlockSpec((D, HALF), lambda r: (0, 2 * n))

    return call(
        row_kernel,
        "row_part",
        flops=6 * 10**9,
        moved=6 * MIB,
        grid=(ROWS_LOCAL,),
        in_specs=[pl.BlockSpec((1, C, D), lambda r: (r, 0, 0)), part(0), part(1), part(2)],
        out_specs=pl.BlockSpec((1, C, HALF), lambda r: (r, 0, 0)),
        out_shape=like(ROWS_LOCAL, C, HALF),
    )(sig, w_qkv, w_qkv, w_qkv)


def columns_of(held, weight, allowed, keep):
    qkv = jnp.dot(held[...], weight, preferred_element_type=F32)
    for c in range(2):

        def store(lo, out):
            keep(c * 256 + lo, out)

        attend(qkv[c * 256 : (c + 1) * 256], allowed, store)


def own_kernel(got_ref, w_ref, held, out_ref):
    pick = one_hot(lambda o: (o % 64) * 2 + o // 64)
    for b in range(4):
        moved = move(pick, got_ref[b * BLOCK : (b + 1) * BLOCK, :])
        held[b * 64 : b * 64 + 64, :] = moved[:64]
        held[256 + b * 64 : 256 + b * 64 + 64, :] = moved[64:]

    def keep(lo, out):
        out_ref[lo : lo + BLOCK, :] = out

    weight = jnp.concatenate(
        [w_ref[:, HALF:256], w_ref[:, 256 + HALF : 512], w_ref[:, 512 + HALF :]], axis=1
    )
    columns_of(held, weight, causal(), keep)


def own_part(got, w_qkv):
    return call(
        own_kernel,
        "own_part",
        flops=10**12,
        moved=4 * MIB,
        in_specs=[whole(), whole()],
        out_specs=[whole(), whole()],
        out_shape=[like(C, D), like(C, HALF)],
    )(got, w_qkv)


def column_kernel(
    meta, held, own, w_out_ref, near, far, out_ref, weights, values, mixers, outs, sems
):
    core = meta[2]
    copies = []

    def fetch(source, target):
        copies.append(pltpu.make_async_copy(source, target, sems.at[len(copies)]))

    for n, d in enumerate((0, 2, 1, 3)):
        for ref, on in ((near, core), (far, 1 - core)):
            at = lax.rem(meta[1] + 4 - d, 4) * 2 + on
            rows = pl.ds(pl.multiple_of(at * BLOCK, BLOCK), BLOCK)
            fetch(ref.at[0, n], weights.at[:, rows, :])
            at = lax.rem(meta[3] + 4 - d, 4) * 2 + on
            rows = pl.ds(pl.multiple_of(at * BLOCK, BLOCK), BLOCK)
            fetch(ref.at[1, n, :, :, :HALF], values.at[:, rows, :])
            fetch(ref.at[1, n, :, :, HALF:], mixers.at[:, at])
    for copy in copies:
        copy.start()
    allowed = causal()
    outs[:, :HALF] = own[...]
    for copy in copies:
        copy.wait()
    for n in range(3):

        def keep(lo, out):
            outs[lo : lo + BLOCK, (n + 1) * HALF : (n + 2) * HALF] = out

        columns_of(held, jnp.concatenate([weights[n], values[n]], axis=1), allowed, keep)
    mixer = jnp.concatenate(
        [w_out_ref[HALF:, :]]
        + [jnp.concatenate([mixers[n, s] for s in range(8)], axis=1) for n in range(3)],
        axis=0,
    )
    back = one_hot(lambda o: (o % 2) * 64 + o // 2)
    for b in range(4):
        both = jnp.concatenate(
            [outs[b * 64 : b * 64 + 64, :], outs[256 + b * 64 : 256 + b * 64 + 64, :]], axis=0
        )
        mixed = jnp.dot(move(back, both), mixer, preferred_element_type=F32).astype(BF)
        for j in range(GROUPS):
            out_ref[b * 16 : (b + 1) * 16, j] = mixed[:, j * 256 : (j + 1) * 256].reshape(16, 8, 256)


def column_part(meta, held, own, w_out, near, far):
    return call(
        column_kernel,
        "column_part",
        flops=3 * 10**9,
        moved=6 * MIB,
        in_specs=[smem(), whole(), whole(), whole(), anywhere(), anywhere()],
        out_specs=whole(),
        out_shape=like(64, GROUPS, 8, 256),
        scratch_shapes=[
            VMEM((3, D, 256), BF),
            VMEM((3, D, HALF), BF),
            VMEM((3, 8, BLOCK, HALF), BF),
            VMEM((C, C), BF),
            pltpu.SemaphoreType.DMA((24,)),
        ],
    )(meta, held, own, w_out, near, far)


def join_kernel(meta, got_ref, rows_ref, w0, w1, w2, w3, out_ref):
    g = meta[0]
    weight = jnp.concatenate([w0[...], w1[...], w2[...], w3[...]], axis=0)
    pick = one_hot(lambda o: ((o // 2) % 16) * 8 + (o // 32) * 2 + o % 2)
    columns = [
        jnp.dot(
            pick,
            got_ref[b * 16 : (b + 1) * 16, 0].reshape(BLOCK, 256),
            preferred_element_type=F32,
        )
        for b in range(4)
    ]
    for r in range(ROWS_LOCAL):
        left = jnp.concatenate(
            [rows_ref[lax.rem(g + GROUPS - k, GROUPS), r, 0] for k in (0,) + ORDER], axis=1
        )
        right = jnp.concatenate([column[r * 32 : (r + 1) * 32] for column in columns], axis=0)
        mixed = jnp.dot(left, weight, preferred_element_type=F32) + right
        out_ref[r, 0] = mixed.astype(BF)


def join(meta, got, rows, w_out, w_rows):
    return call(
        join_kernel,
        "join",
        flops=2 * 10**9,
        moved=4 * MIB,
        grid_spec=pltpu.PrefetchScalarGridSpec(
            num_scalar_prefetch=1,
            grid=(GROUPS,),
            in_specs=[
                pl.BlockSpec((64, 1, 8, 256), lambda j, meta: (0, j, 0, 0)),
                pl.BlockSpec(
                    (GROUPS, ROWS_LOCAL, 1, BLOCK, HALF), lambda j, meta: (0, 0, j, 0, 0)
                ),
                pl.BlockSpec((BLOCK, 256), lambda j, meta: (0, meta[0])),
            ]
            + [pl.BlockSpec((BLOCK, 256), lambda j, meta: (0, 0))] * 3,
            out_specs=pl.BlockSpec((ROWS_LOCAL, 1, BLOCK, 256), lambda j, meta: (0, j, 0, 0)),
        ),
        out_shape=like(ROWS_LOCAL, GROUPS, BLOCK, 256),
    )(meta, got, rows, w_out, *w_rows)


def to_group(data, k):
    return lax.ppermute(data, "heads", [(j, (j + k) % GROUPS) for j in range(GROUPS)])


def along_x(data, d):
    return lax.ppermute(
        data, "rows", [(i, i // 8 * 8 + (i // 2 % 4 + d) % 4 * 2 + i % 2) for i in range(64)]
    )


def along_y(data, d):
    return lax.ppermute(
        data, "rows", [(i, i // 32 * 32 + (i // 8 % 4 + d) % 4 * 8 + i % 8) for i in range(64)]
    )


def other_core(data):
    return lax.ppermute(data, "rows", [(i, i ^ 1) for i in range(64)])


def local(signal, w_qkv, w_out):
    i = lax.axis_index("rows")
    g = lax.axis_index("heads")
    meta = jnp.stack([g, i // 2 % 4, i % 2, i // 8 % 4]).astype(jnp.int32)
    sig = signal.reshape(ROWS_LOCAL, C, D)

    mine, *w_rows = cut(meta, w_qkv, w_out)
    others_x, others_y = mid([to_group(mine, k) for k in ORDER])
    w_rows = [to_group(part, k) for part, k in zip(w_rows, ORDER)]

    send = prep(meta, sig).reshape(64, 8, D)
    got = lax.all_to_all(send, "rows", split_axis=0, concat_axis=0, tiled=True).reshape(C, D)

    own_rows = row_part(sig, w_qkv)
    rows = lax.all_gather(own_rows.reshape(ROWS_LOCAL * C, HALF), "heads", axis=0)

    near = stack(
        [others_x]
        + [along_x(others_x, d) for d in (2, 1, 3)]
        + [others_y]
        + [along_y(others_y, d) for d in (2, 1, 3)],
        [own_rows],
    )
    far = other_core(near)

    held, own = own_part(got, w_qkv)
    columns = column_part(meta, held, own, w_out, near, far).reshape(64 * GROUPS, 8, 256)
    back = lax.all_to_all(columns, ("rows", "heads"), split_axis=0, concat_axis=0, tiled=True)
    return join(
        meta,
        back.reshape(64, GROUPS, 8, 256),
        rows.reshape(GROUPS, ROWS_LOCAL, GROUPS, BLOCK, HALF),
        w_out,
        w_rows,
    ).reshape(ROWS_LOCAL * C, 256)


def solution(mesh):
    return jax.shard_map(
        local,
        mesh=mesh,
        in_specs=(P("rows", None), P(None, "heads"), P("heads", None)),
        out_specs=P("rows", "heads"),
        check_vma=False,
    )
```

```python
import jax
import jax.numpy as jnp
from jax import lax
from jax.experimental import pallas as pl
from jax.experimental.pallas import tpu as pltpu
from jax.sharding import PartitionSpec as P

D = 1024
HEADS = 16
C = 512
GROUPS = 4
DIM = 64
HALF = 128
ROWS_LOCAL = 4
BLOCK = 128
BF = jnp.bfloat16
F32 = jnp.float32
VMEM = pltpu.VMEM
MIB = 1 << 20
ORDER = (2, 1, 3)
SCALE = 0.125 * 1.4426950408889634


def whole():
    return pl.BlockSpec(memory_space=VMEM)


def anywhere():
    return pl.BlockSpec(memory_space=pl.ANY)


def smem():
    return pl.BlockSpec(memory_space=pltpu.SMEM)


def one_hot(source_of):
    out_at = lax.broadcasted_iota(jnp.int32, (BLOCK, BLOCK), 0)
    in_at = lax.broadcasted_iota(jnp.int32, (BLOCK, BLOCK), 1)
    return (in_at == source_of(out_at)).astype(F32).astype(BF)


def move(pick, data):
    return jnp.dot(pick, data, preferred_element_type=F32).astype(BF)


def causal():
    at_query = lax.broadcasted_iota(jnp.int32, (2 * BLOCK, BLOCK), 0) % BLOCK
    return lax.broadcasted_iota(jnp.int32, (2 * BLOCK, BLOCK), 1) <= at_query


def attend(qkv, allowed, store):
    length = qkv.shape[0]
    first = lax.broadcasted_iota(jnp.int32, (1, HALF), 1) < DIM
    query = qkv[:, :HALF]
    query_a = jnp.where(first, query, 0.0).astype(BF)
    query_b = jnp.where(first, 0.0, query).astype(BF)
    key = qkv[:, HALF : 2 * HALF].astype(BF)
    value = qkv[:, 2 * HALF :].astype(BF)
    value = jnp.concatenate([value, jnp.ones((length, HALF), BF)], axis=1)
    for block in range(length // BLOCK):
        lo = block * BLOCK
        hi = lo + BLOCK
        both = jnp.concatenate([query_a[lo:hi], query_b[lo:hi]], axis=0)
        scores = lax.dot_general(
            both, key[:hi], (((1,), (1,)), ((), ())), preferred_element_type=F32
        )
        pieces = [scores[:, n * BLOCK : (n + 1) * BLOCK] for n in range(block)]
        pieces.append(jnp.where(allowed, scores[:, lo:], F32(-1e30)))
        top = pieces[0]
        for piece in pieces[1:]:
            top = jnp.maximum(top, piece)
        top = jnp.max(top, axis=-1, keepdims=True)
        expo = [jnp.exp2((piece - top) * F32(SCALE)).astype(BF) for piece in pieces]
        out = jnp.dot(jnp.concatenate(expo, axis=1), value[:hi], preferred_element_type=F32)
        out = jnp.where(jnp.concatenate([first, first], axis=1), out[:BLOCK], out[BLOCK:])
        store(lo, (out[:, :HALF] / out[:, HALF:]).astype(BF))


def call(kernel, name, flops=0, moved=MIB, vmem=56 * MIB, **options):
    return pl.pallas_call(
        kernel,
        compiler_params=pltpu.CompilerParams(vmem_limit_bytes=vmem),
        cost_estimate=pl.CostEstimate(flops=flops, bytes_accessed=moved, transcendentals=0),
        name=name,
        **options,
    )


def like(*shape):
    return jax.ShapeDtypeStruct(shape, BF)


def cut_kernel(meta, query_ref, key_ref, value_ref, col_ref, out_ref):
    out_ref[:, :HALF] = query_ref[...]
    out_ref[:, HALF : 2 * HALF] = key_ref[...]
    out_ref[:, 2 * HALF : 3 * HALF] = value_ref[...]
    out_ref[:, 3 * HALF :] = col_ref[...]


def cut(meta, w_qkv, w_out):
    def part(n, axis):
        return pl.BlockSpec((BLOCK, HALF), lambda b, meta: (meta[axis] * 2 + meta[2], 2 * n + 1))

    return call(
        cut_kernel,
        "cut",
        grid_spec=pltpu.PrefetchScalarGridSpec(
            num_scalar_prefetch=1,
            grid=(1,),
            in_specs=[
                part(0, 1),
                part(1, 1),
                part(2, 3),
                pl.BlockSpec((BLOCK, HALF), lambda b, meta: (1, meta[3] * 2 + meta[2])),
            ],
            out_specs=pl.BlockSpec((BLOCK, 4 * HALF), lambda b, meta: (0, 0)),
        ),
        out_shape=like(BLOCK, 4 * HALF),
    )(meta, w_qkv, w_qkv, w_qkv, w_out)


def split_kernel(meta, row_ref, *outs):
    for k, ref in zip(ORDER, outs):
        at = pl.multiple_of(lax.rem(meta[0] + k, GROUPS) * 256, 256)
        ref[...] = row_ref[:, pl.ds(at, 256)]


def split(meta, w_out):
    return call(
        split_kernel,
        "split",
        flops=10 * 10**9,
        grid_spec=pltpu.PrefetchScalarGridSpec(
            num_scalar_prefetch=1,
            grid=(1,),
            in_specs=[pl.BlockSpec((BLOCK, D), lambda b, meta: (0, 0))],
            out_specs=[pl.BlockSpec((BLOCK, 256), lambda b, meta: (0, 0))] * 3,
        ),
        out_shape=[like(BLOCK, 256)] * 3,
    )(meta, w_out)


def mid_kernel(in0, in1, in2, x_ref, y_ref):
    for n, ref in enumerate((in0, in1, in2)):
        x_ref[n] = ref[:, :256]
        y_ref[n] = ref[:, 256:]


def mid(parts):
    return call(
        mid_kernel,
        "mid",
        flops=10**12,
        vmem=16 * MIB,
        in_specs=[whole()] * 3,
        out_specs=[whole()] * 2,
        out_shape=[like(3, BLOCK, 256)] * 2,
    )(*parts)


def stack_kernel(*refs):
    out_ref = refs[-1]
    for n in range(8):
        out_ref[n // 4, n % 4] = refs[n][...]


def stack(parts, after):
    return call(
        stack_kernel,
        "stack",
        flops=10**9,
        vmem=16 * MIB,
        in_specs=[whole()] * 8 + [anywhere()] * len(after),
        out_specs=whole(),
        out_shape=like(2, 4, 3, BLOCK, 256),
    )(*parts, *after)


def prep_kernel(meta, sig_ref, after, out_ref):
    pick = one_hot(lambda o: ((o // 2) % 4) * 32 + (o // 8) * 2 + o % 2)
    for b in range(2):
        part = sig_ref[:, b * 32 : (b + 1) * 32, :].reshape(BLOCK, D)
        out_ref[b * BLOCK : (b + 1) * BLOCK, :] = move(pick, part)


def prep(meta, sig, after):
    return call(
        prep_kernel,
        "prep",
        flops=2 * C * D * BLOCK,
        moved=2 * MIB,
        grid_spec=pltpu.PrefetchScalarGridSpec(
            num_scalar_prefetch=1,
            grid=(2,),
            in_specs=[
                pl.BlockSpec((4, 64, D), lambda b, meta: (0, meta[0] * 2 + b, 0)),
                anywhere(),
            ],
            out_specs=pl.BlockSpec((256, D), lambda b, meta: (b, 0)),
        ),
        out_shape=like(C, D),
    )(meta, sig, after)


def row_kernel(sig_ref, query_ref, key_ref, value_ref, out_ref):
    weight = jnp.concatenate([query_ref[...], key_ref[...], value_ref[...]], axis=1)
    qkv = jnp.dot(sig_ref[0], weight, preferred_element_type=F32)

    def store(lo, out):
        out_ref[0, lo : lo + BLOCK, :] = out

    attend(qkv, causal(), store)


def row_part(sig, w_qkv):
    def part(n):
        return pl.BlockSpec((D, HALF), lambda r: (0, 2 * n))

    return call(
        row_kernel,
        "row_part",
        flops=6 * 10**9,
        moved=6 * MIB,
        grid=(ROWS_LOCAL,),
        in_specs=[pl.BlockSpec((1, C, D), lambda r: (r, 0, 0)), part(0), part(1), part(2)],
        out_specs=pl.BlockSpec((1, C, HALF), lambda r: (r, 0, 0)),
        out_shape=like(ROWS_LOCAL, C, HALF),
    )(sig, w_qkv, w_qkv, w_qkv)


def columns_of(held, weight, allowed, keep):
    qkv = jnp.dot(held[...], weight, preferred_element_type=F32)
    for c in range(2):

        def store(lo, out):
            keep(c * 256 + lo, out)

        attend(qkv[c * 256 : (c + 1) * 256], allowed, store)


def own_kernel(got_ref, w_ref, held, out_ref):
    pick = one_hot(lambda o: (o % 64) * 2 + o // 64)
    for b in range(4):
        moved = move(pick, got_ref[b * BLOCK : (b + 1) * BLOCK, :])
        held[b * 64 : b * 64 + 64, :] = moved[:64]
        held[256 + b * 64 : 256 + b * 64 + 64, :] = moved[64:]

    def keep(lo, out):
        out_ref[lo : lo + BLOCK, :] = out

    weight = jnp.concatenate(
        [w_ref[:, HALF:256], w_ref[:, 256 + HALF : 512], w_ref[:, 512 + HALF :]], axis=1
    )
    columns_of(held, weight, causal(), keep)


def own_part(got, w_qkv):
    return call(
        own_kernel,
        "own_part",
        flops=10**12,
        moved=4 * MIB,
        in_specs=[whole(), whole()],
        out_specs=[whole(), whole()],
        out_shape=[like(C, D), like(C, HALF)],
    )(got, w_qkv)


def column_kernel(
    meta, held, own, w_out_ref, near, far, out_ref, weights, values, mixers, outs, sems
):
    core = meta[2]
    copies = []

    def fetch(source, target):
        copies.append(pltpu.make_async_copy(source, target, sems.at[len(copies)]))

    for n, d in enumerate((0, 2, 1, 3)):
        for ref, on in ((near, core), (far, 1 - core)):
            at = lax.rem(meta[1] + 4 - d, 4) * 2 + on
            rows = pl.ds(pl.multiple_of(at * BLOCK, BLOCK), BLOCK)
            fetch(ref.at[0, n], weights.at[:, rows, :])
            at = lax.rem(meta[3] + 4 - d, 4) * 2 + on
            rows = pl.ds(pl.multiple_of(at * BLOCK, BLOCK), BLOCK)
            fetch(ref.at[1, n, :, :, :HALF], values.at[:, rows, :])
            fetch(ref.at[1, n, :, :, HALF:], mixers.at[:, at])
    for copy in copies:
        copy.start()
    allowed = causal()
    outs[:, :HALF] = own[...]
    for copy in copies:
        copy.wait()
    for n in range(3):

        def keep(lo, out):
            outs[lo : lo + BLOCK, (n + 1) * HALF : (n + 2) * HALF] = out

        columns_of(held, jnp.concatenate([weights[n], values[n]], axis=1), allowed, keep)
    mixer = jnp.concatenate(
        [w_out_ref[HALF:, :]]
        + [jnp.concatenate([mixers[n, s] for s in range(8)], axis=1) for n in range(3)],
        axis=0,
    )
    back = one_hot(lambda o: (o % 2) * 64 + o // 2)
    for b in range(4):
        both = jnp.concatenate(
            [outs[b * 64 : b * 64 + 64, :], outs[256 + b * 64 : 256 + b * 64 + 64, :]], axis=0
        )
        mixed = jnp.dot(move(back, both), mixer, preferred_element_type=F32).astype(BF)
        for j in range(GROUPS):
            out_ref[b * 16 : (b + 1) * 16, j] = mixed[:, j * 256 : (j + 1) * 256].reshape(16, 8, 256)


def column_part(meta, held, own, w_out, near, far):
    return call(
        column_kernel,
        "column_part",
        flops=3 * 10**9,
        moved=6 * MIB,
        in_specs=[smem(), whole(), whole(), whole(), anywhere(), anywhere()],
        out_specs=whole(),
        out_shape=like(64, GROUPS, 8, 256),
        scratch_shapes=[
            VMEM((3, D, 256), BF),
            VMEM((3, D, HALF), BF),
            VMEM((3, 8, BLOCK, HALF), BF),
            VMEM((C, C), BF),
            pltpu.SemaphoreType.DMA((24,)),
        ],
    )(meta, held, own, w_out, near, far)


def mix_kernel(meta, rows_ref, w0, w1, w2, w3, out_ref):
    g = meta[0]
    weight = jnp.concatenate([w0[...], w1[...], w2[...], w3[...]], axis=0)
    for r in range(ROWS_LOCAL):
        left = jnp.concatenate(
            [rows_ref[lax.rem(g + GROUPS - k, GROUPS), r, 0] for k in (0,) + ORDER], axis=1
        )
        out_ref[r, 0] = jnp.dot(left, weight, preferred_element_type=F32)


def mix(meta, rows, w_out, w_rows):
    return call(
        mix_kernel,
        "mix",
        flops=2 * 10**9,
        moved=5 * MIB,
        grid_spec=pltpu.PrefetchScalarGridSpec(
            num_scalar_prefetch=1,
            grid=(GROUPS,),
            in_specs=[
                pl.BlockSpec(
                    (GROUPS, ROWS_LOCAL, 1, BLOCK, HALF), lambda j, meta: (0, 0, j, 0, 0)
                ),
                pl.BlockSpec((BLOCK, 256), lambda j, meta: (0, meta[0])),
            ]
            + [pl.BlockSpec((BLOCK, 256), lambda j, meta: (0, 0))] * 3,
            out_specs=pl.BlockSpec((ROWS_LOCAL, 1, BLOCK, 256), lambda j, meta: (0, j, 0, 0)),
        ),
        out_shape=jax.ShapeDtypeStruct((ROWS_LOCAL, GROUPS, BLOCK, 256), F32),
    )(meta, rows, w_out, *w_rows)


def join_kernel(got_ref, rows_ref, out_ref):
    pick = one_hot(lambda o: ((o // 2) % 16) * 8 + (o // 32) * 2 + o % 2)
    for b in range(4):
        moved = jnp.dot(
            pick,
            got_ref[b * 16 : (b + 1) * 16, 0].reshape(BLOCK, 256),
            preferred_element_type=F32,
        )
        for r in range(ROWS_LOCAL):
            lo = b * 32
            out_ref[r, 0, lo : lo + 32] = (
                moved[r * 32 : (r + 1) * 32] + rows_ref[r, 0, lo : lo + 32]
            ).astype(BF)


def join(got, rows):
    block = pl.BlockSpec((ROWS_LOCAL, 1, BLOCK, 256), lambda j: (0, j, 0, 0))
    return call(
        join_kernel,
        "join",
        flops=10**8,
        moved=4 * MIB,
        grid=(GROUPS,),
        in_specs=[pl.BlockSpec((64, 1, 8, 256), lambda j: (0, j, 0, 0)), block],
        out_specs=block,
        out_shape=like(ROWS_LOCAL, GROUPS, BLOCK, 256),
    )(got, rows)


def to_group(data, k):
    return lax.ppermute(data, "heads", [(j, (j + k) % GROUPS) for j in range(GROUPS)])


def along_x(data, d):
    return lax.ppermute(
        data, "rows", [(i, i // 8 * 8 + (i // 2 % 4 + d) % 4 * 2 + i % 2) for i in range(64)]
    )


def along_y(data, d):
    return lax.ppermute(
        data, "rows", [(i, i // 32 * 32 + (i // 8 % 4 + d) % 4 * 8 + i % 8) for i in range(64)]
    )


def other_core(data):
    return lax.ppermute(data, "rows", [(i, i ^ 1) for i in range(64)])


def local(signal, w_qkv, w_out):
    i = lax.axis_index("rows")
    g = lax.axis_index("heads")
    meta = jnp.stack([g, i // 2 % 4, i % 2, i // 8 % 4]).astype(jnp.int32)
    sig = signal.reshape(ROWS_LOCAL, C, D)

    mine = cut(meta, w_qkv, w_out)
    pieces = split(meta, w_out)
    others_x, others_y = mid([to_group(mine, k) for k in ORDER])
    w_rows = [to_group(part, k) for part, k in zip(pieces, ORDER)]

    own_rows = row_part(sig, w_qkv)
    rows = lax.all_gather(own_rows.reshape(ROWS_LOCAL * C, HALF), "heads", axis=0)

    send = prep(meta, sig, own_rows).reshape(64, 8, D)
    got = lax.all_to_all(send, "rows", split_axis=0, concat_axis=0, tiled=True).reshape(C, D)

    near = stack(
        [others_x]
        + [along_x(others_x, d) for d in (2, 1, 3)]
        + [others_y]
        + [along_y(others_y, d) for d in (2, 1, 3)],
        pieces,
    )
    far = other_core(near)

    held, own = own_part(got, w_qkv)
    columns = column_part(meta, held, own, w_out, near, far).reshape(64 * GROUPS, 8, 256)
    back = lax.all_to_all(columns, ("rows", "heads"), split_axis=0, concat_axis=0, tiled=True)
    mixed = mix(meta, rows.reshape(GROUPS, ROWS_LOCAL, GROUPS, BLOCK, HALF), w_out, w_rows)
    return join(back.reshape(64, GROUPS, 8, 256), mixed).reshape(ROWS_LOCAL * C, 256)


def solution(mesh):
    return jax.shard_map(
        local,
        mesh=mesh,
        in_specs=(P("rows", None), P(None, "heads"), P("heads", None)),
        out_specs=P("rows", "heads"),
        check_vma=False,
    )
```

```python
import jax
import jax.numpy as jnp
from jax import lax
from jax.experimental import pallas as pl
from jax.experimental.pallas import tpu as pltpu
from jax.sharding import PartitionSpec as P

D = 1024
HEADS = 16
C = 512
GROUPS = 4
DIM = 64
HALF = 128
ROWS_LOCAL = 4
BLOCK = 128
BF = jnp.bfloat16
F32 = jnp.float32
VMEM = pltpu.VMEM
MIB = 1 << 20
ORDER = (2, 1, 3)
STEPS = (1, 3, 2)
SCALE = 0.125 * 1.4426950408889634


def whole():
    return pl.BlockSpec(memory_space=VMEM)


def anywhere():
    return pl.BlockSpec(memory_space=pl.ANY)


def smem():
    return pl.BlockSpec(memory_space=pltpu.SMEM)


def one_hot(source_of):
    out_at = lax.broadcasted_iota(jnp.int32, (BLOCK, BLOCK), 0)
    in_at = lax.broadcasted_iota(jnp.int32, (BLOCK, BLOCK), 1)
    return (in_at == source_of(out_at)).astype(F32).astype(BF)


def move(pick, data):
    return jnp.dot(pick, data, preferred_element_type=F32).astype(BF)


def causal():
    at_query = lax.broadcasted_iota(jnp.int32, (2 * BLOCK, BLOCK), 0) % BLOCK
    return lax.broadcasted_iota(jnp.int32, (2 * BLOCK, BLOCK), 1) <= at_query


def attend(qkv, allowed, store):
    length = qkv.shape[0]
    first = lax.broadcasted_iota(jnp.int32, (1, HALF), 1) < DIM
    query = qkv[:, :HALF]
    query_a = jnp.where(first, query, 0.0).astype(BF)
    query_b = jnp.where(first, 0.0, query).astype(BF)
    key = qkv[:, HALF : 2 * HALF].astype(BF)
    value = qkv[:, 2 * HALF :].astype(BF)
    value = jnp.concatenate([value, jnp.ones((length, HALF), BF)], axis=1)
    for block in range(length // BLOCK):
        lo = block * BLOCK
        hi = lo + BLOCK
        both = jnp.concatenate([query_a[lo:hi], query_b[lo:hi]], axis=0)
        scores = lax.dot_general(
            both, key[:hi], (((1,), (1,)), ((), ())), preferred_element_type=F32
        )
        pieces = [scores[:, n * BLOCK : (n + 1) * BLOCK] for n in range(block)]
        pieces.append(jnp.where(allowed, scores[:, lo:], F32(-1e30)))
        top = pieces[0]
        for piece in pieces[1:]:
            top = jnp.maximum(top, piece)
        top = jnp.max(top, axis=-1, keepdims=True)
        expo = [jnp.exp2((piece - top) * F32(SCALE)).astype(BF) for piece in pieces]
        out = jnp.dot(jnp.concatenate(expo, axis=1), value[:hi], preferred_element_type=F32)
        out = jnp.where(jnp.concatenate([first, first], axis=1), out[:BLOCK], out[BLOCK:])
        store(lo, (out[:, :HALF] / out[:, HALF:]).astype(BF))


def call(kernel, name, flops=0, moved=MIB, vmem=56 * MIB, **options):
    return pl.pallas_call(
        kernel,
        compiler_params=pltpu.CompilerParams(vmem_limit_bytes=vmem),
        cost_estimate=pl.CostEstimate(flops=flops, bytes_accessed=moved, transcendentals=0),
        name=name,
        **options,
    )


def like(*shape):
    return jax.ShapeDtypeStruct(shape, BF)


def cut_kernel(meta, query_ref, key_ref, value_ref, col_ref, row_ref, *outs):
    for k, out_ref in zip(ORDER, outs):
        out_ref[:, :HALF] = query_ref[...]
        out_ref[:, HALF : 2 * HALF] = key_ref[...]
        out_ref[:, 2 * HALF : 3 * HALF] = value_ref[...]
        out_ref[:, 3 * HALF : 4 * HALF] = col_ref[...]
        at = pl.multiple_of(lax.rem(meta[0] + k, GROUPS) * 256, 256)
        out_ref[:, 4 * HALF :] = row_ref[:, pl.ds(at, 256)]


def cut(meta, w_qkv, w_out):
    def part(n, axis):
        return pl.BlockSpec((BLOCK, HALF), lambda b, meta: (meta[axis] * 2 + meta[2], 2 * n + 1))

    return call(
        cut_kernel,
        "cut",
        grid_spec=pltpu.PrefetchScalarGridSpec(
            num_scalar_prefetch=1,
            grid=(1,),
            in_specs=[
                part(0, 1),
                part(1, 1),
                part(2, 3),
                pl.BlockSpec((BLOCK, HALF), lambda b, meta: (1, meta[3] * 2 + meta[2])),
                pl.BlockSpec((BLOCK, D), lambda b, meta: (0, 0)),
            ],
            out_specs=[pl.BlockSpec((BLOCK, 6 * HALF), lambda b, meta: (0, 0))] * 3,
        ),
        out_shape=[like(BLOCK, 6 * HALF)] * 3,
    )(meta, w_qkv, w_qkv, w_qkv, w_out, w_out)


def mid_kernel(in0, in1, in2, after, x_ref, y_ref, row_ref):
    for n, ref in enumerate((in0, in1, in2)):
        x_ref[n] = ref[:, :256]
        y_ref[n] = ref[:, 256:512]
        row_ref[n * BLOCK : (n + 1) * BLOCK, :] = ref[:, 512:]


def mid(parts, after):
    return call(
        mid_kernel,
        "mid",
        flops=10**12,
        vmem=16 * MIB,
        in_specs=[whole()] * 3 + [anywhere()],
        out_specs=[whole()] * 3,
        out_shape=[like(3, BLOCK, 256)] * 2 + [like(3 * BLOCK, 256)],
    )(*parts, after)


def pick_kernel(query_ref, key_ref, value_ref, out_ref):
    out_ref[:, :HALF] = query_ref[...]
    out_ref[:, HALF : 2 * HALF] = key_ref[...]
    out_ref[:, 2 * HALF :] = value_ref[...]


def pick_columns(w_qkv):
    def part(n):
        return pl.BlockSpec((D, HALF), lambda b: (0, 2 * n + 1))

    return call(
        pick_kernel,
        "pick_columns",
        flops=10**10,
        grid=(1,),
        in_specs=[part(0), part(1), part(2)],
        out_specs=pl.BlockSpec((D, 3 * HALF), lambda b: (0, 0)),
        out_shape=like(D, 3 * HALF),
    )(w_qkv, w_qkv, w_qkv)


def stack_kernel(*refs):
    out_ref = refs[-1]
    for n in range(8):
        out_ref[n // 4, n % 4] = refs[n][...]


def stack(parts, after):
    return call(
        stack_kernel,
        "stack",
        flops=10**9,
        vmem=16 * MIB,
        in_specs=[whole()] * 8 + [anywhere()] * len(after),
        out_specs=whole(),
        out_shape=like(2, 4, 3, BLOCK, 256),
    )(*parts, *after)


def prep_kernel(meta, sig_ref, out_ref):
    pick = one_hot(lambda o: ((o // 2) % 4) * 32 + (o // 8) * 2 + o % 2)
    for b in range(2):
        part = sig_ref[:, b * 32 : (b + 1) * 32, :].reshape(BLOCK, D)
        out_ref[b * BLOCK : (b + 1) * BLOCK, :] = move(pick, part)


def prep(meta, sig):
    return call(
        prep_kernel,
        "prep",
        flops=2 * C * D * BLOCK,
        moved=2 * MIB,
        grid_spec=pltpu.PrefetchScalarGridSpec(
            num_scalar_prefetch=1,
            grid=(2,),
            in_specs=[pl.BlockSpec((4, 64, D), lambda b, meta: (0, meta[0] * 2 + b, 0))],
            out_specs=pl.BlockSpec((256, D), lambda b, meta: (b, 0)),
        ),
        out_shape=like(C, D),
    )(meta, sig)


def row_kernel(sig_ref, query_ref, key_ref, value_ref, after, out_ref, token_ref):
    token_ref[...] = jnp.zeros_like(token_ref)
    weight = jnp.concatenate([query_ref[...], key_ref[...], value_ref[...]], axis=1)
    qkv = jnp.dot(sig_ref[0], weight, preferred_element_type=F32)

    def store(lo, out):
        out_ref[0, lo : lo + BLOCK, :] = out

    attend(qkv, causal(), store)


def row_part(sig, w_qkv, after):
    def part(n):
        return pl.BlockSpec((D, HALF), lambda r: (0, 2 * n))

    return call(
        row_kernel,
        "row_part",
        moved=1,
        grid=(ROWS_LOCAL,),
        in_specs=[pl.BlockSpec((1, C, D), lambda r: (r, 0, 0)), part(0), part(1), part(2), anywhere()],
        out_specs=[
            pl.BlockSpec((1, C, HALF), lambda r: (r, 0, 0)),
            pl.BlockSpec((16, HALF), lambda r: (0, 0)),
        ],
        out_shape=[like(ROWS_LOCAL, C, HALF), like(16, HALF)],
    )(sig, w_qkv, w_qkv, w_qkv, after)


def columns_of(held, weight, allowed, keep):
    qkv = jnp.dot(held[...], weight, preferred_element_type=F32)
    for c in range(2):

        def store(lo, out):
            keep(c * 256 + lo, out)

        attend(qkv[c * 256 : (c + 1) * 256], allowed, store)


def own_kernel(got_ref, w_ref, held, out_ref):
    pick = one_hot(lambda o: (o % 64) * 2 + o // 64)
    for b in range(4):
        moved = move(pick, got_ref[b * BLOCK : (b + 1) * BLOCK, :])
        held[b * 64 : b * 64 + 64, :] = moved[:64]
        held[256 + b * 64 : 256 + b * 64 + 64, :] = moved[64:]

    def keep(lo, out):
        out_ref[lo : lo + BLOCK, :] = out

    columns_of(held, w_ref[...], causal(), keep)


def own_part(got, w_qkv):
    return call(
        own_kernel,
        "own_part",
        flops=10**12,
        moved=4 * MIB,
        in_specs=[whole(), whole()],
        out_specs=[whole(), whole()],
        out_shape=[like(C, D), like(C, HALF)],
    )(got, w_qkv)


def column_kernel(
    meta, held, own, w_out_ref, near, far, out_ref, weights, values, mixers, outs, sems
):
    core = meta[2]
    copies = []

    def fetch(source, target):
        copies.append(pltpu.make_async_copy(source, target, sems.at[len(copies)]))

    for n, d in enumerate((0,) + STEPS):
        for ref, on in ((near, core), (far, 1 - core)):
            at = lax.rem(meta[1] + 4 - d, 4) * 2 + on
            rows = pl.ds(pl.multiple_of(at * BLOCK, BLOCK), BLOCK)
            fetch(ref.at[0, n], weights.at[:, rows, :])
            at = lax.rem(meta[3] + 4 - d, 4) * 2 + on
            rows = pl.ds(pl.multiple_of(at * BLOCK, BLOCK), BLOCK)
            fetch(ref.at[1, n, :, :, :HALF], values.at[:, rows, :])
            fetch(ref.at[1, n, :, :, HALF:], mixers.at[:, at])
    for copy in copies:
        copy.start()
    allowed = causal()
    outs[:, :HALF] = own[...]
    for copy in copies:
        copy.wait()
    for n in range(3):

        def keep(lo, out):
            outs[lo : lo + BLOCK, (n + 1) * HALF : (n + 2) * HALF] = out

        columns_of(held, jnp.concatenate([weights[n], values[n]], axis=1), allowed, keep)
    mixer = jnp.concatenate(
        [w_out_ref[HALF:, :]]
        + [jnp.concatenate([mixers[n, s] for s in range(8)], axis=1) for n in range(3)],
        axis=0,
    )
    back = one_hot(lambda o: (o % 2) * 64 + o // 2)
    for b in range(4):
        both = jnp.concatenate(
            [outs[b * 64 : b * 64 + 64, :], outs[256 + b * 64 : 256 + b * 64 + 64, :]], axis=0
        )
        mixed = jnp.dot(move(back, both), mixer, preferred_element_type=F32).astype(BF)
        for j in range(GROUPS):
            out_ref[b * 16 : (b + 1) * 16, j] = mixed[:, j * 256 : (j + 1) * 256].reshape(16, 8, 256)


def column_part(meta, held, own, w_out, near, far):
    return call(
        column_kernel,
        "column_part",
        flops=3 * 10**9,
        moved=6 * MIB,
        in_specs=[smem(), whole(), whole(), whole(), anywhere(), anywhere()],
        out_specs=whole(),
        out_shape=like(64, GROUPS, 8, 256),
        scratch_shapes=[
            VMEM((3, D, 256), BF),
            VMEM((3, D, HALF), BF),
            VMEM((3, 8, BLOCK, HALF), BF),
            VMEM((C, C), BF),
            pltpu.SemaphoreType.DMA((24,)),
        ],
    )(meta, held, own, w_out, near, far)


def mix_kernel(meta, rows_ref, own_ref, w_ref, out_ref):
    g = meta[0]
    weight = jnp.concatenate([own_ref[...], w_ref[...]], axis=0)
    for r in range(ROWS_LOCAL):
        left = jnp.concatenate(
            [rows_ref[lax.rem(g + GROUPS - k, GROUPS), r, 0] for k in (0,) + ORDER], axis=1
        )
        out_ref[r, 0] = jnp.dot(left, weight, preferred_element_type=F32)


def mix(meta, rows, w_out, w_rows):
    return call(
        mix_kernel,
        "mix",
        flops=2 * 10**9,
        moved=5 * MIB,
        grid_spec=pltpu.PrefetchScalarGridSpec(
            num_scalar_prefetch=1,
            grid=(GROUPS,),
            in_specs=[
                pl.BlockSpec(
                    (GROUPS, ROWS_LOCAL, 1, BLOCK, HALF), lambda j, meta: (0, 0, j, 0, 0)
                ),
                pl.BlockSpec((BLOCK, 256), lambda j, meta: (0, meta[0])),
                pl.BlockSpec((3 * BLOCK, 256), lambda j, meta: (0, 0)),
            ],
            out_specs=pl.BlockSpec((ROWS_LOCAL, 1, BLOCK, 256), lambda j, meta: (0, j, 0, 0)),
        ),
        out_shape=jax.ShapeDtypeStruct((ROWS_LOCAL, GROUPS, BLOCK, 256), F32),
    )(meta, rows, w_out, w_rows)


def join_kernel(got_ref, rows_ref, out_ref):
    pick = one_hot(lambda o: ((o // 2) % 16) * 8 + (o // 32) * 2 + o % 2)
    for b in range(4):
        moved = jnp.dot(
            pick,
            got_ref[b * 16 : (b + 1) * 16, 0].reshape(BLOCK, 256),
            preferred_element_type=F32,
        )
        for r in range(ROWS_LOCAL):
            lo = b * 32
            out_ref[r, 0, lo : lo + 32] = (
                moved[r * 32 : (r + 1) * 32] + rows_ref[r, 0, lo : lo + 32]
            ).astype(BF)


def join(got, rows):
    block = pl.BlockSpec((ROWS_LOCAL, 1, BLOCK, 256), lambda j: (0, j, 0, 0))
    return call(
        join_kernel,
        "join",
        vmem=16 * MIB,
        flops=10**8,
        moved=4 * MIB,
        grid=(GROUPS,),
        in_specs=[pl.BlockSpec((64, 1, 8, 256), lambda j: (0, j, 0, 0)), block],
        out_specs=block,
        out_shape=like(ROWS_LOCAL, GROUPS, BLOCK, 256),
    )(got, rows)


def to_group(data, k):
    return lax.ppermute(data, "heads", [(j, (j + k) % GROUPS) for j in range(GROUPS)])


def along_x(data, d):
    return lax.ppermute(
        data, "rows", [(i, i // 8 * 8 + (i // 2 % 4 + d) % 4 * 2 + i % 2) for i in range(64)]
    )


def along_y(data, d):
    return lax.ppermute(
        data, "rows", [(i, i // 32 * 32 + (i // 8 % 4 + d) % 4 * 8 + i % 8) for i in range(64)]
    )


def other_core(data):
    return lax.ppermute(data, "rows", [(i, i ^ 1) for i in range(64)])


def local(signal, w_qkv, w_out):
    i = lax.axis_index("rows")
    g = lax.axis_index("heads")
    meta = jnp.stack([g, i // 2 % 4, i % 2, i // 8 % 4]).astype(jnp.int32)
    sig = signal.reshape(ROWS_LOCAL, C, D)

    send = prep(meta, sig)
    own_rows, rows_done = row_part(sig, w_qkv, send)
    send = send.reshape(64, 8, D)
    got = lax.all_to_all(send, "rows", split_axis=0, concat_axis=0, tiled=True).reshape(C, D)
    rows = lax.all_gather(own_rows.reshape(ROWS_LOCAL * C, HALF), "heads", axis=0)

    cuts = cut(meta, w_qkv, w_out)
    cuts = [to_group(part, k) for part, k in zip(cuts, ORDER)]
    others_x, others_y, w_rows = mid(cuts, rows_done)
    w_own = pick_columns(w_qkv)

    near = stack(
        [others_x]
        + [along_x(others_x, d) for d in STEPS]
        + [others_y]
        + [along_y(others_y, d) for d in STEPS],
        [w_own],
    )
    far = other_core(near)

    held, own = own_part(got, w_own)
    columns = column_part(meta, held, own, w_out, near, far).reshape(64 * GROUPS, 8, 256)
    back = lax.all_to_all(columns, ("rows", "heads"), split_axis=0, concat_axis=0, tiled=True)
    mixed = mix(meta, rows.reshape(GROUPS, ROWS_LOCAL, GROUPS, BLOCK, HALF), w_out, w_rows)
    return join(back.reshape(64, GROUPS, 8, 256), mixed).reshape(ROWS_LOCAL * C, 256)


def solution(mesh):
    return jax.shard_map(
        local,
        mesh=mesh,
        in_specs=(P("rows", None), P(None, "heads"), P("heads", None)),
        out_specs=P("rows", "heads"),
        check_vma=False,
    )
```

```python
import jax
import jax.numpy as jnp
from jax import lax
from jax.experimental import pallas as pl
from jax.experimental.pallas import tpu as pltpu
from jax.sharding import PartitionSpec as P

D = 1024
HEADS = 16
C = 512
GROUPS = 4
DIM = 64
HALF = 128
ROWS_LOCAL = 4
BLOCK = 128
BF = jnp.bfloat16
F32 = jnp.float32
VMEM = pltpu.VMEM
MIB = 1 << 20
ORDER = (3, 1, 2)
STEPS = (2, 3, 1)
WIDE = 5 * HALF
BOTH = ("rows", "heads")
SCALE = 0.125 * 1.4426950408889634


def whole():
    return pl.BlockSpec(memory_space=VMEM)


def anywhere():
    return pl.BlockSpec(memory_space=pl.ANY)


def smem():
    return pl.BlockSpec(memory_space=pltpu.SMEM)


def one_hot(source_of):
    out_at = lax.broadcasted_iota(jnp.int32, (BLOCK, BLOCK), 0)
    in_at = lax.broadcasted_iota(jnp.int32, (BLOCK, BLOCK), 1)
    return (in_at == source_of(out_at)).astype(F32).astype(BF)


def move(pick, data):
    return jnp.dot(pick, data, preferred_element_type=F32).astype(BF)


def causal():
    at_query = lax.broadcasted_iota(jnp.int32, (2 * BLOCK, BLOCK), 0) % BLOCK
    return lax.broadcasted_iota(jnp.int32, (2 * BLOCK, BLOCK), 1) <= at_query


def attend(qkv, allowed, store):
    length = qkv.shape[0]
    first = lax.broadcasted_iota(jnp.int32, (1, HALF), 1) < DIM
    query = qkv[:, :HALF]
    query_a = jnp.where(first, query, 0.0).astype(BF)
    query_b = jnp.where(first, 0.0, query).astype(BF)
    key = qkv[:, HALF : 2 * HALF].astype(BF)
    value = qkv[:, 2 * HALF :].astype(BF)
    value = jnp.concatenate([value, jnp.ones((length, HALF), BF)], axis=1)
    for block in range(length // BLOCK):
        lo = block * BLOCK
        hi = lo + BLOCK
        both = jnp.concatenate([query_a[lo:hi], query_b[lo:hi]], axis=0)
        scores = lax.dot_general(
            both, key[:hi], (((1,), (1,)), ((), ())), preferred_element_type=F32
        )
        pieces = [scores[:, n * BLOCK : (n + 1) * BLOCK] for n in range(block)]
        pieces.append(jnp.where(allowed, scores[:, lo:], F32(-1e30)))
        top = pieces[0]
        for piece in pieces[1:]:
            top = jnp.maximum(top, piece)
        top = jnp.max(top, axis=-1, keepdims=True)
        expo = [jnp.exp2((piece - top) * F32(SCALE)).astype(BF) for piece in pieces]
        out = jnp.dot(jnp.concatenate(expo, axis=1), value[:hi], preferred_element_type=F32)
        out = jnp.where(jnp.concatenate([first, first], axis=1), out[:BLOCK], out[BLOCK:])
        store(lo, (out[:, :HALF] / out[:, HALF:]).astype(BF))


def call(kernel, name, flops=0, moved=MIB, vmem=56 * MIB, **options):
    return pl.pallas_call(
        kernel,
        compiler_params=pltpu.CompilerParams(vmem_limit_bytes=vmem),
        cost_estimate=pl.CostEstimate(flops=flops, bytes_accessed=moved, transcendentals=0),
        name=name,
        **options,
    )


def like(*shape):
    return jax.ShapeDtypeStruct(shape, BF)


def cut_kernel(meta, query_ref, key_ref, value_ref, mix_ref, out_ref):
    out_ref[:, :HALF] = query_ref[...]
    out_ref[:, HALF : 2 * HALF] = key_ref[...]
    out_ref[:, 2 * HALF : 3 * HALF] = value_ref[...]
    out_ref[:, 3 * HALF : 4 * HALF] = mix_ref[HALF:, :]
    out_ref[:, 4 * HALF :] = mix_ref[:HALF, :]


def cut(meta, w_qkv, w_out):
    def part(n, axis):
        return pl.BlockSpec((BLOCK, HALF), lambda b, meta: (meta[axis] * 2 + meta[2], 2 * n + 1))

    return call(
        cut_kernel,
        "cut",
        grid_spec=pltpu.PrefetchScalarGridSpec(
            num_scalar_prefetch=1,
            grid=(1,),
            in_specs=[
                part(0, 1),
                part(1, 1),
                part(2, 3),
                pl.BlockSpec((256, BLOCK), lambda b, meta: (0, meta[3] * 2 + meta[2])),
            ],
            out_specs=pl.BlockSpec((BLOCK, WIDE), lambda b, meta: (0, 0)),
        ),
        out_shape=like(BLOCK, WIDE),
    )(meta, w_qkv, w_qkv, w_qkv, w_out)


def mid_kernel(in0, in1, in2, x_ref, y_ref):
    for n, ref in enumerate((in0, in1, in2)):
        x_ref[n] = ref[:, :256]
        y_ref[n] = ref[:, 256:]


def mid(parts):
    return call(
        mid_kernel,
        "mid",
        flops=10**12,
        vmem=16 * MIB,
        in_specs=[whole()] * 3,
        out_specs=[whole()] * 2,
        out_shape=[like(3, BLOCK, 256), like(3, BLOCK, WIDE - 256)],
    )(*parts)


def stack_kernel(*refs):
    out_ref = refs[-1]
    for d in range(4):
        for n in range(3):
            out_ref[n, d, :, :256] = refs[d][n]
            out_ref[n, d, :, 256:] = refs[4 + d][n]


def stack(parts, after):
    return call(
        stack_kernel,
        "stack",
        flops=10**9,
        vmem=16 * MIB,
        in_specs=[whole()] * 8 + [anywhere()] * len(after),
        out_specs=whole(),
        out_shape=like(3, 4, BLOCK, WIDE),
    )(*parts, *after)


def prep_kernel(meta, sig_ref, out_ref):
    pick = one_hot(lambda o: ((o // 2) % 4) * 32 + (o // 8) * 2 + o % 2)
    for b in range(2):
        part = sig_ref[:, b * 32 : (b + 1) * 32, :].reshape(BLOCK, D)
        out_ref[b * BLOCK : (b + 1) * BLOCK, :] = move(pick, part)


def prep(meta, sig):
    return call(
        prep_kernel,
        "prep",
        flops=2 * C * D * BLOCK,
        moved=2 * MIB,
        grid_spec=pltpu.PrefetchScalarGridSpec(
            num_scalar_prefetch=1,
            grid=(2,),
            in_specs=[pl.BlockSpec((4, 64, D), lambda b, meta: (0, meta[0] * 2 + b, 0))],
            out_specs=pl.BlockSpec((256, D), lambda b, meta: (b, 0)),
        ),
        out_shape=like(C, D),
    )(meta, sig)


def row_kernel(sig_ref, query_ref, key_ref, value_ref, after, out_ref, token_ref, held):
    r = pl.program_id(0)
    weight = jnp.concatenate([query_ref[...], key_ref[...], value_ref[...]], axis=1)
    qkv = jnp.dot(sig_ref[0], weight, preferred_element_type=F32)

    def store(lo, out):
        held[r, lo : lo + BLOCK, :] = out

    attend(qkv, causal(), store)

    @pl.when(r == ROWS_LOCAL - 1)
    def _():
        token_ref[...] = jnp.zeros_like(token_ref)
        pick = one_hot(lambda o: ((o // 2) % 4) * 32 + (o // 8) * 2 + o % 2)
        for j in range(GROUPS):
            for b in range(4):
                lo = j * BLOCK + b * 32
                part = held[:, lo : lo + 32, :].reshape(BLOCK, HALF)
                out_ref[b * 16 : (b + 1) * 16, j] = move(pick, part).reshape(16, 8, HALF)


def row_part(sig, w_qkv, after):
    def part(n):
        return pl.BlockSpec((D, HALF), lambda r: (0, 2 * n))

    return call(
        row_kernel,
        "row_part",
        flops=10**10,
        moved=1,
        grid=(ROWS_LOCAL,),
        in_specs=[
            pl.BlockSpec((1, C, D), lambda r: (r, 0, 0)),
            part(0),
            part(1),
            part(2),
            anywhere(),
        ],
        out_specs=[
            pl.BlockSpec((64, GROUPS, 8, HALF), lambda r: (0, 0, 0, 0)),
            pl.BlockSpec((16, HALF), lambda r: (0, 0)),
        ],
        out_shape=[like(64, GROUPS, 8, HALF), like(16, HALF)],
        scratch_shapes=[VMEM((ROWS_LOCAL, C, HALF), BF)],
    )(sig, w_qkv, w_qkv, w_qkv, after)


def columns_of(qkv, allowed, keep):
    for c in range(2):

        def store(lo, out):
            keep(c * 256 + lo, out)

        attend(qkv[c * 256 : (c + 1) * 256], allowed, store)


def own_kernel(meta, got_ref, w_qkv, by_x, by_y, out_ref, held, weight, sems):
    copies = [
        pltpu.make_async_copy(
            w_qkv.at[:, 256 * n + HALF : 256 * (n + 1)],
            weight.at[:, HALF * n : HALF * (n + 1)],
            sems.at[n],
        )
        for n in range(3)
    ]
    for copy in copies:
        copy.start()
    pick = one_hot(lambda o: (o % 64) * 2 + o // 64)
    for b in range(4):
        moved = move(pick, got_ref[b * BLOCK : (b + 1) * BLOCK, :])
        held[b * 64 : b * 64 + 64, :] = moved[:64]
        held[256 + b * 64 : 256 + b * 64 + 64, :] = moved[64:]
    core = meta[2]
    for n, d in enumerate((0,) + STEPS):
        for far, on in enumerate((core, 1 - core)):
            lo = (4 * far + n) * BLOCK
            for at, out in ((meta[1], by_x), (meta[3], by_y)):
                source = pl.multiple_of((lax.rem(at + 4 - d, 4) * 2 + on) * BLOCK, BLOCK)
                out[:, lo : lo + BLOCK] = held[:, pl.ds(source, BLOCK)]

    def keep(lo, out):
        out_ref[lo : lo + BLOCK, :] = out

    for copy in copies:
        copy.wait()
    qkv = jnp.dot(held[...], weight[...], preferred_element_type=F32)
    columns_of(qkv, causal(), keep)


def own_part(meta, got, w_qkv):
    return call(
        own_kernel,
        "own_part",
        flops=10**12,
        moved=4 * MIB,
        vmem=20 * MIB,
        in_specs=[smem(), whole(), anywhere()],
        out_specs=[whole()] * 3,
        out_shape=[like(C, D), like(C, D), like(C, HALF)],
        scratch_shapes=[
            VMEM((C, D), BF),
            VMEM((D, 3 * HALF), BF),
            pltpu.SemaphoreType.DMA((3,)),
        ],
    )(meta, got, w_qkv)


def column_kernel(by_x, by_y, own, near, far, out_ref, outs):
    allowed = causal()
    outs[:, :HALF] = own[...]
    half = 4 * BLOCK
    for n in range(3):

        def keep(lo, out):
            outs[lo : lo + BLOCK, (n + 1) * HALF : (n + 2) * HALF] = out

        def product(left, lanes):
            return jnp.dot(
                left[:, :half],
                near[n, :, :, lanes].reshape(half, -1),
                preferred_element_type=F32,
            ) + jnp.dot(
                left[:, half:],
                far[n, :, :, lanes].reshape(half, -1),
                preferred_element_type=F32,
            )

        qkv = jnp.concatenate(
            [product(by_x, slice(0, 256)), product(by_y, slice(256, 256 + HALF))], axis=1
        )
        columns_of(qkv, allowed, keep)
    back = one_hot(lambda o: (o % 2) * 64 + o // 2)
    for b in range(4):
        both = jnp.concatenate(
            [outs[b * 64 : b * 64 + 64, :], outs[256 + b * 64 : 256 + b * 64 + 64, :]], axis=0
        )
        out_ref[b * BLOCK : (b + 1) * BLOCK, :] = move(back, both)


def column_part(by_x, by_y, own, near, far):
    return call(
        column_kernel,
        "column_part",
        flops=3 * 10**9,
        moved=6 * MIB,
        vmem=20 * MIB,
        in_specs=[whole()] * 5,
        out_specs=whole(),
        out_shape=like(C, C),
        scratch_shapes=[VMEM((C, C), BF)],
    )(by_x, by_y, own, near, far)


def mix_kernel(meta, columns, rows, w_out, near, far, out_ref):
    core = meta[2]
    left = jnp.concatenate(
        [columns[...]]
        + [
            rows[:, lax.rem(meta[0] + GROUPS - k, GROUPS)].reshape(C, HALF)
            for k in (0,) + ORDER
        ],
        axis=1,
    )
    for n, d in enumerate((0,) + STEPS):
        j = lax.rem(meta[3] + 4 - d, 4)
        own = w_out[:, pl.ds(pl.multiple_of(j * 256, 256), 256)]
        parts = []
        for lo, mine in ((3 * HALF, own[HALF:]), (4 * HALF, own[:HALF])):
            here = near[:, n, :, lo : lo + HALF].reshape(3 * BLOCK, HALF)
            there = far[:, n, :, lo : lo + HALF].reshape(3 * BLOCK, HALF)
            low = jnp.where(core == 0, here, there)
            high = jnp.where(core == 0, there, here)
            parts += [mine, jnp.concatenate([low, high], axis=1)]
        mixed = jnp.dot(left, jnp.concatenate(parts, axis=0), preferred_element_type=F32)
        out_ref[:, j] = mixed.astype(BF).reshape(64, 8, 256)


def mix(meta, columns, rows, w_out, near, far):
    return call(
        mix_kernel,
        "mix",
        flops=10**9,
        moved=6 * MIB,
        vmem=20 * MIB,
        in_specs=[smem()] + [whole()] * 5,
        out_specs=whole(),
        out_shape=like(64, GROUPS, 8, 256),
    )(meta, columns, rows, w_out, near, far)


def join_kernel(got_ref, out_ref):
    pick = one_hot(lambda o: ((o // 2) % 16) * 8 + (o // 32) * 2 + o % 2)
    for b in range(4):
        moved = move(pick, got_ref[b * 16 : (b + 1) * 16, 0].reshape(BLOCK, 256))
        for r in range(ROWS_LOCAL):
            out_ref[r, 0, b * 32 : (b + 1) * 32] = moved[r * 32 : (r + 1) * 32]


def join(got):
    return call(
        join_kernel,
        "join",
        flops=10**8,
        moved=4 * MIB,
        vmem=16 * MIB,
        grid=(GROUPS,),
        in_specs=[pl.BlockSpec((64, 1, 8, 256), lambda j: (0, j, 0, 0))],
        out_specs=pl.BlockSpec((ROWS_LOCAL, 1, BLOCK, 256), lambda j: (0, j, 0, 0)),
        out_shape=like(ROWS_LOCAL, GROUPS, BLOCK, 256),
    )(got)


def to_group(data, k):
    return lax.ppermute(data, "heads", [(j, (j + k) % GROUPS) for j in range(GROUPS)])


def along_x(data, d):
    return lax.ppermute(
        data, "rows", [(i, i // 8 * 8 + (i // 2 % 4 + d) % 4 * 2 + i % 2) for i in range(64)]
    )


def along_y(data, d):
    return lax.ppermute(
        data, "rows", [(i, i // 32 * 32 + (i // 8 % 4 + d) % 4 * 8 + i % 8) for i in range(64)]
    )


def other_core(data):
    return lax.ppermute(data, "rows", [(i, i ^ 1) for i in range(64)])


def local(signal, w_qkv, w_out):
    i = lax.axis_index("rows")
    g = lax.axis_index("heads")
    meta = jnp.stack([g, i // 2 % 4, i % 2, i // 8 % 4]).astype(jnp.int32)
    sig = signal.reshape(ROWS_LOCAL, C, D)

    send = prep(meta, sig)
    own_rows, rows_done = row_part(sig, w_qkv, send)
    got = lax.all_to_all(
        send.reshape(64, 8, D), "rows", split_axis=0, concat_axis=0, tiled=True
    ).reshape(C, D)
    rows = lax.all_to_all(
        own_rows.reshape(64 * GROUPS, 8, HALF), BOTH, split_axis=0, concat_axis=0, tiled=True
    ).reshape(64, GROUPS, 8, HALF)

    mine = cut(meta, w_qkv, w_out)
    others_x, others_y = mid([to_group(mine, k) for k in ORDER])
    near = stack(
        [others_x]
        + [along_x(others_x, d) for d in STEPS]
        + [others_y]
        + [along_y(others_y, d) for d in STEPS],
        [rows_done, got],
    )
    far = other_core(near)

    by_x, by_y, own = own_part(meta, got, w_qkv)
    columns = column_part(by_x, by_y, own, near, far)
    mixed = mix(meta, columns, rows, w_out, near, far).reshape(64 * GROUPS, 8, 256)
    back = lax.all_to_all(mixed, BOTH, split_axis=0, concat_axis=0, tiled=True)
    return join(back.reshape(64, GROUPS, 8, 256)).reshape(ROWS_LOCAL * C, 256)


def solution(mesh):
    return jax.shard_map(
        local,
        mesh=mesh,
        in_specs=(P("rows", None), P(None, "heads"), P("heads", None)),
        out_specs=P("rows", "heads"),
        check_vma=False,
    )
```

```python
import jax
import jax.numpy as jnp
from jax import lax
from jax.experimental import pallas as pl
from jax.experimental.pallas import tpu as pltpu
from jax.sharding import PartitionSpec as P

D = 1024
HEADS = 16
C = 512
GROUPS = 4
DIM = 64
HALF = 128
ROWS_LOCAL = 4
BLOCK = 128
BF = jnp.bfloat16
F32 = jnp.float32
VMEM = pltpu.VMEM
MIB = 1 << 20
ORDER = (3, 1, 2)
STEPS = (2, 3, 1)
WIDE = 5 * HALF
BOTH = ("rows", "heads")
SCALE = 0.125 * 1.4426950408889634


def whole():
    return pl.BlockSpec(memory_space=VMEM)


def anywhere():
    return pl.BlockSpec(memory_space=pl.ANY)


def smem():
    return pl.BlockSpec(memory_space=pltpu.SMEM)


def one_hot(source_of):
    out_at = lax.broadcasted_iota(jnp.int32, (BLOCK, BLOCK), 0)
    in_at = lax.broadcasted_iota(jnp.int32, (BLOCK, BLOCK), 1)
    return (in_at == source_of(out_at)).astype(F32).astype(BF)


def move(pick, data):
    return jnp.dot(pick, data, preferred_element_type=F32).astype(BF)


def causal():
    at_query = lax.broadcasted_iota(jnp.int32, (2 * BLOCK, BLOCK), 0) % BLOCK
    return lax.broadcasted_iota(jnp.int32, (2 * BLOCK, BLOCK), 1) <= at_query


def attend(qkv, allowed, store):
    length = qkv.shape[0]
    first = lax.broadcasted_iota(jnp.int32, (1, HALF), 1) < DIM
    query = qkv[:, :HALF]
    query_a = jnp.where(first, query, 0.0).astype(BF)
    query_b = jnp.where(first, 0.0, query).astype(BF)
    key = qkv[:, HALF : 2 * HALF].astype(BF)
    value = qkv[:, 2 * HALF :].astype(BF)
    value = jnp.concatenate([value, jnp.ones((length, HALF), BF)], axis=1)
    for block in range(length // BLOCK):
        lo = block * BLOCK
        hi = lo + BLOCK
        both = jnp.concatenate([query_a[lo:hi], query_b[lo:hi]], axis=0)
        scores = lax.dot_general(
            both, key[:hi], (((1,), (1,)), ((), ())), preferred_element_type=F32
        )
        pieces = [scores[:, n * BLOCK : (n + 1) * BLOCK] for n in range(block)]
        pieces.append(jnp.where(allowed, scores[:, lo:], F32(-1e30)))
        top = pieces[0]
        for piece in pieces[1:]:
            top = jnp.maximum(top, piece)
        top = jnp.max(top, axis=-1, keepdims=True)
        expo = [jnp.exp2((piece - top) * F32(SCALE)).astype(BF) for piece in pieces]
        out = jnp.dot(jnp.concatenate(expo, axis=1), value[:hi], preferred_element_type=F32)
        out = jnp.where(jnp.concatenate([first, first], axis=1), out[:BLOCK], out[BLOCK:])
        store(lo, (out[:, :HALF] / out[:, HALF:]).astype(BF))


def call(kernel, name, flops=0, moved=MIB, vmem=56 * MIB, **options):
    return pl.pallas_call(
        kernel,
        compiler_params=pltpu.CompilerParams(vmem_limit_bytes=vmem),
        cost_estimate=pl.CostEstimate(flops=flops, bytes_accessed=moved, transcendentals=0),
        name=name,
        **options,
    )


def like(*shape):
    return jax.ShapeDtypeStruct(shape, BF)


def cut_kernel(meta, query_ref, key_ref, value_ref, mix_ref, out_ref):
    out_ref[:, :HALF] = query_ref[...]
    out_ref[:, HALF : 2 * HALF] = key_ref[...]
    out_ref[:, 2 * HALF : 3 * HALF] = value_ref[...]
    out_ref[:, 3 * HALF : 5 * HALF] = mix_ref[HALF:, :]
    out_ref[:, 5 * HALF :] = mix_ref[:HALF, :]


def cut(meta, w_qkv, w_out):
    def part(n):
        return pl.BlockSpec((BLOCK, HALF), lambda b, meta: (meta[1] * 2 + meta[2], 2 * n + 1))

    return call(
        cut_kernel,
        "cut",
        grid_spec=pltpu.PrefetchScalarGridSpec(
            num_scalar_prefetch=1,
            grid=(1,),
            in_specs=[
                part(0),
                part(1),
                part(2),
                pl.BlockSpec((256, 256), lambda b, meta: (0, meta[3] * 2 + meta[2])),
            ],
            out_specs=pl.BlockSpec((BLOCK, 7 * HALF), lambda b, meta: (0, 0)),
        ),
        out_shape=like(BLOCK, 7 * HALF),
    )(meta, w_qkv, w_qkv, w_qkv, w_out)


def mid_kernel(in0, in1, in2, after, x_ref, y_ref):
    for n, ref in enumerate((in0, in1, in2)):
        x_ref[n] = ref[:, : 3 * HALF]
        y_ref[n] = ref[:, 3 * HALF :]


def mid(parts, after):
    return call(
        mid_kernel,
        "mid",
        flops=10**12,
        vmem=16 * MIB,
        in_specs=[whole()] * 3 + [anywhere()],
        out_specs=[whole()] * 2,
        out_shape=[like(3, BLOCK, 3 * HALF), like(3, BLOCK, 4 * HALF)],
    )(*parts, after)


def stack_kernel(in0, in1, in2, in3, y0, y1, after, out_ref):
    for n in range(3):
        for d, ref in enumerate((in0, in1, in2, in3)):
            out_ref[n, d, :, : 3 * HALF] = ref[n]
        for d, ref in enumerate((y0, y1)):
            out_ref[n, 2 * d, :, 3 * HALF :] = ref[n, :, :256]
            out_ref[n, 2 * d + 1, :, 3 * HALF :] = ref[n, :, 256:]


def stack(parts, after):
    return call(
        stack_kernel,
        "stack",
        flops=10**9,
        vmem=16 * MIB,
        in_specs=[whole()] * 6 + [anywhere()],
        out_specs=whole(),
        out_shape=like(3, 4, BLOCK, WIDE),
    )(*parts, after)


def prep_kernel(meta, sig_ref, out_ref):
    pick = one_hot(lambda o: ((o // 2) % 4) * 32 + (o // 8) * 2 + o % 2)
    for b in range(2):
        part = sig_ref[:, b * 32 : (b + 1) * 32, :].reshape(BLOCK, D)
        out_ref[b * BLOCK : (b + 1) * BLOCK, :] = move(pick, part)


def prep(meta, sig):
    return call(
        prep_kernel,
        "prep",
        flops=2 * C * D * BLOCK,
        moved=2 * MIB,
        grid_spec=pltpu.PrefetchScalarGridSpec(
            num_scalar_prefetch=1,
            grid=(2,),
            in_specs=[pl.BlockSpec((4, 64, D), lambda b, meta: (0, meta[0] * 2 + b, 0))],
            out_specs=pl.BlockSpec((256, D), lambda b, meta: (b, 0)),
        ),
        out_shape=like(C, D),
    )(meta, sig)


def row_kernel(sig_ref, query_ref, key_ref, value_ref, after, out_ref, token_ref, held):
    r = pl.program_id(0)
    weight = jnp.concatenate([query_ref[...], key_ref[...], value_ref[...]], axis=1)
    qkv = jnp.dot(sig_ref[0], weight, preferred_element_type=F32)

    def store(lo, out):
        held[r, lo : lo + BLOCK, :] = out

    attend(qkv, causal(), store)

    @pl.when(r == ROWS_LOCAL - 1)
    def _():
        token_ref[...] = jnp.zeros_like(token_ref)
        pick = one_hot(lambda o: ((o // 2) % 4) * 32 + (o // 8) * 2 + o % 2)
        for j in range(GROUPS):
            for b in range(4):
                lo = j * BLOCK + b * 32
                part = held[:, lo : lo + 32, :].reshape(BLOCK, HALF)
                out_ref[b * 16 : (b + 1) * 16, j] = move(pick, part).reshape(16, 8, HALF)


def row_part(sig, w_qkv, after):
    def part(n):
        return pl.BlockSpec((D, HALF), lambda r: (0, 2 * n))

    return call(
        row_kernel,
        "row_part",
        moved=1,
        grid=(ROWS_LOCAL,),
        in_specs=[
            pl.BlockSpec((1, C, D), lambda r: (r, 0, 0)),
            part(0),
            part(1),
            part(2),
            anywhere(),
        ],
        out_specs=[
            pl.BlockSpec((64, GROUPS, 8, HALF), lambda r: (0, 0, 0, 0)),
            pl.BlockSpec((16, HALF), lambda r: (0, 0)),
        ],
        out_shape=[like(64, GROUPS, 8, HALF), like(16, HALF)],
        scratch_shapes=[VMEM((ROWS_LOCAL, C, HALF), BF)],
    )(sig, w_qkv, w_qkv, w_qkv, after)


def columns_of(qkv, allowed, keep):
    for c in range(2):

        def store(lo, out):
            keep(c * 256 + lo, out)

        attend(qkv[c * 256 : (c + 1) * 256], allowed, store)


def own_kernel(meta, got_ref, w_qkv, by_x, out_ref, held, weight, sems):
    copies = [
        pltpu.make_async_copy(
            w_qkv.at[:, 256 * n + HALF : 256 * (n + 1)],
            weight.at[:, HALF * n : HALF * (n + 1)],
            sems.at[n],
        )
        for n in range(3)
    ]
    for copy in copies:
        copy.start()
    pick = one_hot(lambda o: (o % 64) * 2 + o // 64)
    for b in range(4):
        moved = move(pick, got_ref[b * BLOCK : (b + 1) * BLOCK, :])
        held[b * 64 : b * 64 + 64, :] = moved[:64]
        held[256 + b * 64 : 256 + b * 64 + 64, :] = moved[64:]
    core = meta[2]
    for n, d in enumerate((0,) + STEPS):
        for far, on in enumerate((core, 1 - core)):
            lo = (4 * far + n) * BLOCK
            source = pl.multiple_of((lax.rem(meta[1] + 4 - d, 4) * 2 + on) * BLOCK, BLOCK)
            by_x[:, lo : lo + BLOCK] = held[:, pl.ds(source, BLOCK)]

    def keep(lo, out):
        out_ref[lo : lo + BLOCK, :] = out

    for copy in copies:
        copy.wait()
    qkv = jnp.dot(held[...], weight[...], preferred_element_type=F32)
    columns_of(qkv, causal(), keep)


def own_part(meta, got, w_qkv):
    return call(
        own_kernel,
        "own_part",
        flops=10**12,
        moved=4 * MIB,
        vmem=20 * MIB,
        in_specs=[smem(), whole(), anywhere()],
        out_specs=[whole()] * 2,
        out_shape=[like(C, D), like(C, HALF)],
        scratch_shapes=[
            VMEM((C, D), BF),
            VMEM((D, 3 * HALF), BF),
            pltpu.SemaphoreType.DMA((3,)),
        ],
    )(meta, got, w_qkv)


def column_kernel(by_x, own, near, far, out_ref, outs):
    allowed = causal()
    outs[:, :HALF] = own[...]
    half = 4 * BLOCK
    for n in range(3):

        def keep(lo, out):
            outs[lo : lo + BLOCK, (n + 1) * HALF : (n + 2) * HALF] = out

        qkv = jnp.dot(
            by_x[:, :half],
            near[n, :, :, : 3 * HALF].reshape(half, 3 * HALF),
            preferred_element_type=F32,
        ) + jnp.dot(
            by_x[:, half:],
            far[n, :, :, : 3 * HALF].reshape(half, 3 * HALF),
            preferred_element_type=F32,
        )
        columns_of(qkv, allowed, keep)
    back = one_hot(lambda o: (o % 2) * 64 + o // 2)
    for b in range(4):
        both = jnp.concatenate(
            [outs[b * 64 : b * 64 + 64, :], outs[256 + b * 64 : 256 + b * 64 + 64, :]], axis=0
        )
        out_ref[b * BLOCK : (b + 1) * BLOCK, :] = move(back, both)


def column_part(by_x, own, near, far):
    return call(
        column_kernel,
        "column_part",
        flops=3 * 10**9,
        moved=6 * MIB,
        vmem=20 * MIB,
        in_specs=[whole()] * 4,
        out_specs=whole(),
        out_shape=like(C, C),
        scratch_shapes=[VMEM((C, C), BF)],
    )(by_x, own, near, far)


def mix_kernel(meta, columns, rows, w_out, near, far, out_ref):
    core = meta[2]
    left = jnp.concatenate(
        [columns[...]]
        + [
            rows[:, lax.rem(meta[0] + GROUPS - k, GROUPS)].reshape(C, HALF)
            for k in (0,) + ORDER
        ],
        axis=1,
    )
    for source, on in ((near, core), (far, 1 - core)):
        for d, y in enumerate((meta[3], 1 - meta[3])):
            j = y * 2 + on
            own = w_out[:, pl.ds(pl.multiple_of(j * 256, 256), 256)]
            weight = jnp.concatenate(
                [
                    own[HALF:],
                    source[:, 2 * d, :, 3 * HALF :].reshape(3 * BLOCK, 256),
                    own[:HALF],
                    source[:, 2 * d + 1, :, 3 * HALF :].reshape(3 * BLOCK, 256),
                ],
                axis=0,
            )
            mixed = jnp.dot(left, weight, preferred_element_type=F32)
            out_ref[:, j] = mixed.astype(BF).reshape(64, 8, 256)


def mix(meta, columns, rows, w_out, near, far):
    return call(
        mix_kernel,
        "mix",
        flops=10**9,
        moved=6 * MIB,
        vmem=20 * MIB,
        in_specs=[smem()] + [whole()] * 5,
        out_specs=whole(),
        out_shape=like(64, GROUPS, 8, 256),
    )(meta, columns, rows, w_out, near, far)


def join_kernel(got_ref, out_ref):
    pick = one_hot(lambda o: ((o // 2) % 16) * 8 + (o // 32) * 2 + o % 2)
    for b in range(4):
        moved = move(pick, got_ref[b * 16 : (b + 1) * 16, 0].reshape(BLOCK, 256))
        for r in range(ROWS_LOCAL):
            out_ref[r, 0, b * 32 : (b + 1) * 32] = moved[r * 32 : (r + 1) * 32]


def join(got):
    return call(
        join_kernel,
        "join",
        flops=10**8,
        moved=4 * MIB,
        vmem=16 * MIB,
        grid=(GROUPS,),
        in_specs=[pl.BlockSpec((64, 1, 8, 256), lambda j: (0, j, 0, 0))],
        out_specs=pl.BlockSpec((ROWS_LOCAL, 1, BLOCK, 256), lambda j: (0, j, 0, 0)),
        out_shape=like(ROWS_LOCAL, GROUPS, BLOCK, 256),
    )(got)


def to_group(data, k):
    return lax.ppermute(data, "heads", [(j, (j + k) % GROUPS) for j in range(GROUPS)])


def along_x(data, d):
    return lax.ppermute(
        data, "rows", [(i, i // 8 * 8 + (i // 2 % 4 + d) % 4 * 2 + i % 2) for i in range(64)]
    )


def other_y(data):
    return lax.ppermute(data, "rows", [(i, i ^ 8) for i in range(64)])


def other_core(data):
    return lax.ppermute(data, "rows", [(i, i ^ 1) for i in range(64)])


def local(signal, w_qkv, w_out):
    i = lax.axis_index("rows")
    g = lax.axis_index("heads")
    meta = jnp.stack([g, i // 2 % 4, i % 2, i // 8 % 2]).astype(jnp.int32)
    sig = signal.reshape(ROWS_LOCAL, C, D)

    send = prep(meta, sig)
    own_rows, rows_done = row_part(sig, w_qkv, send)
    got = lax.all_to_all(
        send.reshape(64, 8, D), "rows", split_axis=0, concat_axis=0, tiled=True
    ).reshape(C, D)
    rows = lax.all_to_all(
        own_rows.reshape(64 * GROUPS, 8, HALF), BOTH, split_axis=0, concat_axis=0, tiled=True
    ).reshape(64, GROUPS, 8, HALF)

    mine = cut(meta, w_qkv, w_out)
    others, blocks = mid([to_group(mine, k) for k in ORDER], rows_done)
    near = stack(
        [others] + [along_x(others, d) for d in STEPS] + [blocks, other_y(blocks)], got
    )
    far = other_core(near)

    by_x, own = own_part(meta, got, w_qkv)
    columns = column_part(by_x, own, near, far)
    mixed = mix(meta, columns, rows, w_out, near, far).reshape(64 * GROUPS, 8, 256)
    back = lax.all_to_all(mixed, BOTH, split_axis=0, concat_axis=0, tiled=True)
    return join(back.reshape(64, GROUPS, 8, 256)).reshape(ROWS_LOCAL * C, 256)


def solution(mesh):
    return jax.shard_map(
        local,
        mesh=mesh,
        in_specs=(P("rows", None), P(None, "heads"), P("heads", None)),
        out_specs=P("rows", "heads"),
        check_vma=False,
    )
```

```python
import jax
import jax.numpy as jnp
from jax import lax
from jax.experimental import pallas as pl
from jax.experimental.pallas import tpu as pltpu
from jax.sharding import PartitionSpec as P

D = 1024
HEADS = 16
C = 512
GROUPS = 4
DIM = 64
HALF = 128
ROWS_LOCAL = 4
BLOCK = 128
BF = jnp.bfloat16
F32 = jnp.float32
VMEM = pltpu.VMEM
MIB = 1 << 20
ORDER = (2, 1, 3)
STEPS = (2, 3, 1)
WIDE = 5 * HALF
BOTH = ("rows", "heads")
SCALE = 0.125 * 1.4426950408889634


def whole():
    return pl.BlockSpec(memory_space=VMEM)


def anywhere():
    return pl.BlockSpec(memory_space=pl.ANY)


def smem():
    return pl.BlockSpec(memory_space=pltpu.SMEM)


def one_hot(source_of):
    out_at = lax.broadcasted_iota(jnp.int32, (BLOCK, BLOCK), 0)
    in_at = lax.broadcasted_iota(jnp.int32, (BLOCK, BLOCK), 1)
    return (in_at == source_of(out_at)).astype(F32).astype(BF)


def move(pick, data):
    return jnp.dot(pick, data, preferred_element_type=F32).astype(BF)


def causal():
    at_query = lax.broadcasted_iota(jnp.int32, (2 * BLOCK, BLOCK), 0) % BLOCK
    return lax.broadcasted_iota(jnp.int32, (2 * BLOCK, BLOCK), 1) <= at_query


def attend(qkv, allowed, store):
    length = qkv.shape[0]
    first = lax.broadcasted_iota(jnp.int32, (1, HALF), 1) < DIM
    query = qkv[:, :HALF]
    query_a = jnp.where(first, query, 0.0).astype(BF)
    query_b = jnp.where(first, 0.0, query).astype(BF)
    key = qkv[:, HALF : 2 * HALF].astype(BF)
    value = qkv[:, 2 * HALF :].astype(BF)
    value = jnp.concatenate([value, jnp.ones((length, HALF), BF)], axis=1)
    for block in range(length // BLOCK):
        lo = block * BLOCK
        hi = lo + BLOCK
        both = jnp.concatenate([query_a[lo:hi], query_b[lo:hi]], axis=0)
        scores = lax.dot_general(
            both, key[:hi], (((1,), (1,)), ((), ())), preferred_element_type=F32
        )
        pieces = [scores[:, n * BLOCK : (n + 1) * BLOCK] for n in range(block)]
        pieces.append(jnp.where(allowed, scores[:, lo:], F32(-1e30)))
        top = pieces[0]
        for piece in pieces[1:]:
            top = jnp.maximum(top, piece)
        top = jnp.max(top, axis=-1, keepdims=True)
        expo = [jnp.exp2((piece - top) * F32(SCALE)).astype(BF) for piece in pieces]
        out = jnp.dot(jnp.concatenate(expo, axis=1), value[:hi], preferred_element_type=F32)
        out = jnp.where(jnp.concatenate([first, first], axis=1), out[:BLOCK], out[BLOCK:])
        store(lo, (out[:, :HALF] / out[:, HALF:]).astype(BF))


def call(kernel, name, flops=0, moved=MIB, vmem=56 * MIB, **options):
    return pl.pallas_call(
        kernel,
        compiler_params=pltpu.CompilerParams(vmem_limit_bytes=vmem),
        cost_estimate=pl.CostEstimate(flops=flops, bytes_accessed=moved, transcendentals=0),
        name=name,
        **options,
    )


def like(*shape):
    return jax.ShapeDtypeStruct(shape, BF)


def cut_kernel(meta, query_ref, key_ref, value_ref, mix_ref, out_ref):
    out_ref[:, :HALF] = query_ref[...]
    out_ref[:, HALF : 2 * HALF] = key_ref[...]
    out_ref[:, 2 * HALF : 3 * HALF] = value_ref[...]
    out_ref[:, 3 * HALF : 5 * HALF] = mix_ref[HALF:, :]
    out_ref[:, 5 * HALF :] = mix_ref[:HALF, :]


def cut(meta, w_qkv, w_out):
    def part(n):
        return pl.BlockSpec((BLOCK, HALF), lambda b, meta: (meta[1] * 2 + meta[2], 2 * n + 1))

    return call(
        cut_kernel,
        "cut",
        grid_spec=pltpu.PrefetchScalarGridSpec(
            num_scalar_prefetch=1,
            grid=(1,),
            in_specs=[
                part(0),
                part(1),
                part(2),
                pl.BlockSpec((256, 256), lambda b, meta: (0, meta[3] * 2 + meta[2])),
            ],
            out_specs=pl.BlockSpec((BLOCK, 7 * HALF), lambda b, meta: (0, 0)),
        ),
        out_shape=like(BLOCK, 7 * HALF),
    )(meta, w_qkv, w_qkv, w_qkv, w_out)


def mid_kernel(in0, in1, in2, after, x_ref, y_ref):
    for n, ref in enumerate((in0, in1, in2)):
        x_ref[n] = ref[:, : 3 * HALF]
        y_ref[n] = ref[:, 3 * HALF :]


def mid(parts, after):
    return call(
        mid_kernel,
        "mid",
        flops=10**12,
        vmem=16 * MIB,
        in_specs=[whole()] * 3 + [anywhere()],
        out_specs=[whole()] * 2,
        out_shape=[like(3, BLOCK, 3 * HALF), like(3, BLOCK, 4 * HALF)],
    )(*parts, after)


def stack_kernel(in0, in1, in2, in3, block0, block1, after, out_ref, blocks_ref):
    for d, ref in enumerate((in0, in1, in2, in3)):
        for n in range(3):
            out_ref[n, d] = ref[n]
    blocks_ref[0] = block0[...]
    blocks_ref[1] = block1[...]


def stack(parts, after):
    return call(
        stack_kernel,
        "stack",
        flops=10**9,
        vmem=16 * MIB,
        in_specs=[whole()] * 6 + [anywhere()],
        out_specs=[whole()] * 2,
        out_shape=[like(3, 4, BLOCK, 3 * HALF), like(2, 3, BLOCK, 4 * HALF)],
    )(*parts, after)


def prep_kernel(meta, sig_ref, out_ref):
    pick = one_hot(lambda o: ((o // 2) % 4) * 32 + (o // 8) * 2 + o % 2)
    for b in range(2):
        part = sig_ref[:, b * 32 : (b + 1) * 32, :].reshape(BLOCK, D)
        out_ref[b * BLOCK : (b + 1) * BLOCK, :] = move(pick, part)


def prep(meta, sig):
    return call(
        prep_kernel,
        "prep",
        flops=2 * C * D * BLOCK,
        moved=2 * MIB,
        grid_spec=pltpu.PrefetchScalarGridSpec(
            num_scalar_prefetch=1,
            grid=(2,),
            in_specs=[pl.BlockSpec((4, 64, D), lambda b, meta: (0, meta[0] * 2 + b, 0))],
            out_specs=pl.BlockSpec((256, D), lambda b, meta: (b, 0)),
        ),
        out_shape=like(C, D),
    )(meta, sig)


def row_kernel(sig_ref, query_ref, key_ref, value_ref, after, out_ref, token_ref, held):
    r = pl.program_id(0)
    weight = jnp.concatenate([query_ref[...], key_ref[...], value_ref[...]], axis=1)
    qkv = jnp.dot(sig_ref[0], weight, preferred_element_type=F32)

    def store(lo, out):
        held[r, lo : lo + BLOCK, :] = out

    attend(qkv, causal(), store)

    @pl.when(r == ROWS_LOCAL - 1)
    def _():
        token_ref[...] = jnp.zeros_like(token_ref)
        pick = one_hot(lambda o: ((o // 2) % 4) * 32 + (o // 8) * 2 + o % 2)
        for j in range(GROUPS):
            for b in range(4):
                lo = j * BLOCK + b * 32
                part = held[:, lo : lo + 32, :].reshape(BLOCK, HALF)
                out_ref[b * 16 : (b + 1) * 16, j] = move(pick, part).reshape(16, 8, HALF)


def row_part(sig, w_qkv, after):
    def part(n):
        return pl.BlockSpec((D, HALF), lambda r: (0, 2 * n))

    return call(
        row_kernel,
        "row_part",
        moved=1,
        grid=(ROWS_LOCAL,),
        in_specs=[
            pl.BlockSpec((1, C, D), lambda r: (r, 0, 0)),
            part(0),
            part(1),
            part(2),
            anywhere(),
        ],
        out_specs=[
            pl.BlockSpec((64, GROUPS, 8, HALF), lambda r: (0, 0, 0, 0)),
            pl.BlockSpec((16, HALF), lambda r: (0, 0)),
        ],
        out_shape=[like(64, GROUPS, 8, HALF), like(16, HALF)],
        scratch_shapes=[VMEM((ROWS_LOCAL, C, HALF), BF)],
    )(sig, w_qkv, w_qkv, w_qkv, after)


def columns_of(qkv, allowed, keep):
    for c in range(2):

        def store(lo, out):
            keep(c * 256 + lo, out)

        attend(qkv[c * 256 : (c + 1) * 256], allowed, store)


def own_kernel(meta, got_ref, w_qkv, by_x, out_ref, held, weight, sems):
    copies = [
        pltpu.make_async_copy(
            w_qkv.at[:, 256 * n + HALF : 256 * (n + 1)],
            weight.at[:, HALF * n : HALF * (n + 1)],
            sems.at[n],
        )
        for n in range(3)
    ]
    for copy in copies:
        copy.start()
    pick = one_hot(lambda o: (o % 64) * 2 + o // 64)
    for b in range(4):
        moved = move(pick, got_ref[b * BLOCK : (b + 1) * BLOCK, :])
        held[b * 64 : b * 64 + 64, :] = moved[:64]
        held[256 + b * 64 : 256 + b * 64 + 64, :] = moved[64:]
    core = meta[2]
    for n, d in enumerate((0,) + STEPS):
        for far, on in enumerate((core, 1 - core)):
            lo = (4 * far + n) * BLOCK
            source = pl.multiple_of((lax.rem(meta[1] + 4 - d, 4) * 2 + on) * BLOCK, BLOCK)
            by_x[:, lo : lo + BLOCK] = held[:, pl.ds(source, BLOCK)]

    def keep(lo, out):
        out_ref[lo : lo + BLOCK, :] = out

    for copy in copies:
        copy.wait()
    qkv = jnp.dot(held[...], weight[...], preferred_element_type=F32)
    columns_of(qkv, causal(), keep)


def own_part(meta, got, w_qkv):
    return call(
        own_kernel,
        "own_part",
        flops=10**12,
        moved=4 * MIB,
        vmem=20 * MIB,
        in_specs=[smem(), whole(), anywhere()],
        out_specs=[whole()] * 2,
        out_shape=[like(C, D), like(C, HALF)],
        scratch_shapes=[
            VMEM((C, D), BF),
            VMEM((D, 3 * HALF), BF),
            pltpu.SemaphoreType.DMA((3,)),
        ],
    )(meta, got, w_qkv)


def column_kernel(by_x, own, near, far, out_ref, near_v, far_v, outs, sems):
    copies = []
    for n in range(3):
        copies.append(pltpu.make_async_copy(near.at[n], near_v.at[n], sems.at[2 * n]))
        copies.append(pltpu.make_async_copy(far.at[n], far_v.at[n], sems.at[2 * n + 1]))
    for copy in copies:
        copy.start()
    allowed = causal()
    outs[:, :HALF] = own[...]
    half = 4 * BLOCK
    for n in range(3):

        def keep(lo, out):
            outs[lo : lo + BLOCK, (n + 1) * HALF : (n + 2) * HALF] = out

        copies[2 * n].wait()
        copies[2 * n + 1].wait()
        qkv = jnp.dot(
            by_x[:, :half], near_v[n].reshape(half, 3 * HALF), preferred_element_type=F32
        ) + jnp.dot(by_x[:, half:], far_v[n].reshape(half, 3 * HALF), preferred_element_type=F32)
        columns_of(qkv, allowed, keep)
    back = one_hot(lambda o: (o % 2) * 64 + o // 2)
    for b in range(4):
        both = jnp.concatenate(
            [outs[b * 64 : b * 64 + 64, :], outs[256 + b * 64 : 256 + b * 64 + 64, :]], axis=0
        )
        out_ref[b * BLOCK : (b + 1) * BLOCK, :] = move(back, both)


def column_part(by_x, own, near, far):
    return call(
        column_kernel,
        "column_part",
        flops=3 * 10**9,
        moved=6 * MIB,
        vmem=20 * MIB,
        in_specs=[whole()] * 2 + [anywhere()] * 2,
        out_specs=whole(),
        out_shape=like(C, C),
        scratch_shapes=[
            VMEM((3, 4, BLOCK, 3 * HALF), BF),
            VMEM((3, 4, BLOCK, 3 * HALF), BF),
            VMEM((C, C), BF),
            pltpu.SemaphoreType.DMA((6,)),
        ],
    )(by_x, own, near, far)


def mix_kernel(meta, columns, rows, w_out, near, far, out_ref):
    core = meta[2]
    y = meta[3]
    left = jnp.concatenate(
        [columns[...]]
        + [
            rows[:, lax.rem(meta[0] + GROUPS - k, GROUPS)].reshape(C, HALF)
            for k in (0,) + ORDER
        ],
        axis=1,
    )
    blocks = (
        (near, 0, y * 2 + core),
        (near, 1, (1 - y) * 2 + core),
        (far, 0, y * 2 + 1 - core),
        (far, 1, (1 - y) * 2 + 1 - core),
    )
    for source, n, j in blocks:
        own = w_out[:, pl.ds(pl.multiple_of(j * 256, 256), 256)]
        weight = jnp.concatenate(
            [
                own[HALF:],
                source[n, :, :, :256].reshape(3 * BLOCK, 256),
                own[:HALF],
                source[n, :, :, 256:].reshape(3 * BLOCK, 256),
            ],
            axis=0,
        )
        mixed = jnp.dot(left, weight, preferred_element_type=F32)
        out_ref[:, j] = mixed.astype(BF).reshape(64, 8, 256)


def mix(meta, columns, rows, w_out, near, far):
    return call(
        mix_kernel,
        "mix",
        flops=10**9,
        moved=6 * MIB,
        vmem=20 * MIB,
        in_specs=[smem()] + [whole()] * 5,
        out_specs=whole(),
        out_shape=like(64, GROUPS, 8, 256),
    )(meta, columns, rows, w_out, near, far)


def join_kernel(got_ref, out_ref):
    pick = one_hot(lambda o: ((o // 2) % 16) * 8 + (o // 32) * 2 + o % 2)
    for b in range(4):
        moved = move(pick, got_ref[b * 16 : (b + 1) * 16, 0].reshape(BLOCK, 256))
        for r in range(ROWS_LOCAL):
            out_ref[r, 0, b * 32 : (b + 1) * 32] = moved[r * 32 : (r + 1) * 32]


def join(got):
    return call(
        join_kernel,
        "join",
        flops=10**8,
        moved=4 * MIB,
        vmem=16 * MIB,
        grid=(GROUPS,),
        in_specs=[pl.BlockSpec((64, 1, 8, 256), lambda j: (0, j, 0, 0))],
        out_specs=pl.BlockSpec((ROWS_LOCAL, 1, BLOCK, 256), lambda j: (0, j, 0, 0)),
        out_shape=like(ROWS_LOCAL, GROUPS, BLOCK, 256),
    )(got)


def to_group(data, k):
    return lax.ppermute(data, "heads", [(j, (j + k) % GROUPS) for j in range(GROUPS)])


def along_x(data, d):
    return lax.ppermute(
        data, "rows", [(i, i // 8 * 8 + (i // 2 % 4 + d) % 4 * 2 + i % 2) for i in range(64)]
    )


def other_y(data):
    return lax.ppermute(data, "rows", [(i, i ^ 8) for i in range(64)])


def other_core(data):
    return lax.ppermute(data, "rows", [(i, i ^ 1) for i in range(64)])


def local(signal, w_qkv, w_out):
    i = lax.axis_index("rows")
    g = lax.axis_index("heads")
    meta = jnp.stack([g, i // 2 % 4, i % 2, i // 8 % 2]).astype(jnp.int32)
    sig = signal.reshape(ROWS_LOCAL, C, D)

    send = prep(meta, sig)
    own_rows, rows_done = row_part(sig, w_qkv, send)
    got = lax.all_to_all(
        send.reshape(64, 8, D), "rows", split_axis=0, concat_axis=0, tiled=True
    ).reshape(C, D)
    rows = lax.all_to_all(
        own_rows.reshape(64 * GROUPS, 8, HALF), BOTH, split_axis=0, concat_axis=0, tiled=True
    ).reshape(64, GROUPS, 8, HALF)

    mine = cut(meta, w_qkv, w_out)
    others, blocks = mid([to_group(mine, k) for k in ORDER], rows_done)
    near, blocks = stack(
        [others] + [along_x(others, d) for d in STEPS] + [blocks, other_y(blocks)], got
    )
    far = other_core(near)
    far_blocks = other_core(blocks)

    by_x, own = own_part(meta, got, w_qkv)
    columns = column_part(by_x, own, near, far)
    mixed = mix(meta, columns, rows, w_out, blocks, far_blocks).reshape(64 * GROUPS, 8, 256)
    back = lax.all_to_all(mixed, BOTH, split_axis=0, concat_axis=0, tiled=True)
    return join(back.reshape(64, GROUPS, 8, 256)).reshape(ROWS_LOCAL * C, 256)


def solution(mesh):
    return jax.shard_map(
        local,
        mesh=mesh,
        in_specs=(P("rows", None), P(None, "heads"), P("heads", None)),
        out_specs=P("rows", "heads"),
        check_vma=False,
    )
```

```python
import jax
import jax.numpy as jnp
from jax import lax
from jax.experimental import pallas as pl
from jax.experimental.pallas import tpu as pltpu
from jax.sharding import PartitionSpec as P

D = 1024
HEADS = 16
C = 512
GROUPS = 4
DIM = 64
HALF = 128
ROWS_LOCAL = 4
BLOCK = 128
BF = jnp.bfloat16
F32 = jnp.float32
VMEM = pltpu.VMEM
MIB = 1 << 20
ORDER = (2, 1, 3)
STEPS = (2, 3, 1)
WIDE = 5 * HALF
BOTH = ("rows", "heads")
SCALE = 0.125 * 1.4426950408889634


def whole():
    return pl.BlockSpec(memory_space=VMEM)


def anywhere():
    return pl.BlockSpec(memory_space=pl.ANY)


def smem():
    return pl.BlockSpec(memory_space=pltpu.SMEM)


def group_of(meta):
    return meta[0] & 3


def x_of(meta):
    return (meta[0] >> 3) & 3


def core_of(meta):
    return (meta[0] >> 2) & 1


def y_of(meta):
    return (meta[0] >> 5) & 1


def one_hot(source_of):
    out_at = lax.broadcasted_iota(jnp.int32, (BLOCK, BLOCK), 0)
    in_at = lax.broadcasted_iota(jnp.int32, (BLOCK, BLOCK), 1)
    return (in_at == source_of(out_at)).astype(F32).astype(BF)


def move(pick, data):
    return jnp.dot(pick, data, preferred_element_type=F32).astype(BF)


def causal():
    at_query = lax.broadcasted_iota(jnp.int32, (2 * BLOCK, BLOCK), 0) % BLOCK
    return lax.broadcasted_iota(jnp.int32, (2 * BLOCK, BLOCK), 1) <= at_query


def attend(qkv, allowed, store):
    length = qkv.shape[0]
    first = lax.broadcasted_iota(jnp.int32, (1, HALF), 1) < DIM
    query = qkv[:, :HALF]
    query_a = jnp.where(first, query, 0.0).astype(BF)
    query_b = jnp.where(first, 0.0, query).astype(BF)
    key = qkv[:, HALF : 2 * HALF].astype(BF)
    value = qkv[:, 2 * HALF :].astype(BF)
    value = jnp.concatenate([value, jnp.ones((length, HALF), BF)], axis=1)
    for block in range(length // BLOCK):
        lo = block * BLOCK
        hi = lo + BLOCK
        both = jnp.concatenate([query_a[lo:hi], query_b[lo:hi]], axis=0)
        scores = lax.dot_general(
            both, key[:hi], (((1,), (1,)), ((), ())), preferred_element_type=F32
        )
        pieces = [scores[:, n * BLOCK : (n + 1) * BLOCK] for n in range(block)]
        pieces.append(jnp.where(allowed, scores[:, lo:], F32(-1e30)))
        top = pieces[0]
        for piece in pieces[1:]:
            top = jnp.maximum(top, piece)
        top = jnp.max(top, axis=-1, keepdims=True)
        expo = [jnp.exp2((piece - top) * F32(SCALE)).astype(BF) for piece in pieces]
        out = jnp.dot(jnp.concatenate(expo, axis=1), value[:hi], preferred_element_type=F32)
        out = jnp.where(jnp.concatenate([first, first], axis=1), out[:BLOCK], out[BLOCK:])
        store(lo, (out[:, :HALF] / out[:, HALF:]).astype(BF))


def call(kernel, name, flops=0, moved=MIB, vmem=56 * MIB, **options):
    return pl.pallas_call(
        kernel,
        compiler_params=pltpu.CompilerParams(vmem_limit_bytes=vmem),
        cost_estimate=pl.CostEstimate(flops=flops, bytes_accessed=moved, transcendentals=0),
        name=name,
        **options,
    )


def like(*shape):
    return jax.ShapeDtypeStruct(shape, BF)


def cut_kernel(meta, query_ref, key_ref, value_ref, mix_ref, out_ref):
    out_ref[:, :HALF] = query_ref[...]
    out_ref[:, HALF : 2 * HALF] = key_ref[...]
    out_ref[:, 2 * HALF : 3 * HALF] = value_ref[...]
    out_ref[:, 3 * HALF : 5 * HALF] = mix_ref[HALF:, :]
    out_ref[:, 5 * HALF :] = mix_ref[:HALF, :]


def cut(meta, w_qkv, w_out):
    def part(n):
        return pl.BlockSpec((BLOCK, HALF), lambda b, meta: (x_of(meta) * 2 + core_of(meta), 2 * n + 1))

    return call(
        cut_kernel,
        "cut",
        grid_spec=pltpu.PrefetchScalarGridSpec(
            num_scalar_prefetch=1,
            grid=(1,),
            in_specs=[
                part(0),
                part(1),
                part(2),
                pl.BlockSpec((256, 256), lambda b, meta: (0, y_of(meta) * 2 + core_of(meta))),
            ],
            out_specs=pl.BlockSpec((BLOCK, 7 * HALF), lambda b, meta: (0, 0)),
        ),
        out_shape=like(BLOCK, 7 * HALF),
    )(meta, w_qkv, w_qkv, w_qkv, w_out)


def mid_kernel(in0, in1, in2, after, x_ref, y_ref):
    for n, ref in enumerate((in0, in1, in2)):
        x_ref[n] = ref[:, : 3 * HALF]
        y_ref[n] = ref[:, 3 * HALF :]


def mid(parts, after):
    return call(
        mid_kernel,
        "mid",
        flops=10**12,
        vmem=16 * MIB,
        in_specs=[whole()] * 3 + [anywhere()],
        out_specs=[whole()] * 2,
        out_shape=[like(3, BLOCK, 3 * HALF), like(3, BLOCK, 4 * HALF)],
    )(*parts, after)


def stack_kernel(in0, in1, in2, in3, block0, block1, after, out_ref, blocks_ref):
    for d, ref in enumerate((in0, in1, in2, in3)):
        for n in range(3):
            out_ref[n, d] = ref[n]
    blocks_ref[0] = block0[...]
    blocks_ref[1] = block1[...]


def stack(parts, after):
    return call(
        stack_kernel,
        "stack",
        flops=10**9,
        vmem=16 * MIB,
        in_specs=[whole()] * 6 + [anywhere()],
        out_specs=[whole()] * 2,
        out_shape=[like(3, 4, BLOCK, 3 * HALF), like(2, 3, BLOCK, 4 * HALF)],
    )(*parts, after)


def prep_kernel(meta, sig_ref, out_ref):
    pick = one_hot(lambda o: ((o // 2) % 4) * 32 + (o // 8) * 2 + o % 2)
    for b in range(2):
        part = sig_ref[:, b * 32 : (b + 1) * 32, :].reshape(BLOCK, D)
        out_ref[b * BLOCK : (b + 1) * BLOCK, :] = move(pick, part)


def prep(meta, sig):
    return call(
        prep_kernel,
        "prep",
        flops=2 * C * D * BLOCK,
        moved=2 * MIB,
        grid_spec=pltpu.PrefetchScalarGridSpec(
            num_scalar_prefetch=1,
            grid=(2,),
            in_specs=[pl.BlockSpec((4, 64, D), lambda b, meta: (0, group_of(meta) * 2 + b, 0))],
            out_specs=pl.BlockSpec((256, D), lambda b, meta: (b, 0)),
        ),
        out_shape=like(C, D),
    )(meta, sig)


def row_kernel(sig_ref, query_ref, key_ref, value_ref, after, out_ref, token_ref, held):
    r = pl.program_id(0)
    weight = jnp.concatenate([query_ref[...], key_ref[...], value_ref[...]], axis=1)
    qkv = jnp.dot(sig_ref[0], weight, preferred_element_type=F32)

    def store(lo, out):
        held[r, lo : lo + BLOCK, :] = out

    attend(qkv, causal(), store)

    @pl.when(r == ROWS_LOCAL - 1)
    def _():
        token_ref[...] = jnp.zeros_like(token_ref)
        pick = one_hot(lambda o: ((o // 2) % 4) * 32 + (o // 8) * 2 + o % 2)
        for j in range(GROUPS):
            for b in range(4):
                lo = j * BLOCK + b * 32
                part = held[:, lo : lo + 32, :].reshape(BLOCK, HALF)
                out_ref[b * 16 : (b + 1) * 16, j] = move(pick, part).reshape(16, 8, HALF)


def row_part(sig, w_qkv, after):
    def part(n):
        return pl.BlockSpec((D, HALF), lambda r: (0, 2 * n))

    return call(
        row_kernel,
        "row_part",
        moved=1,
        grid=(ROWS_LOCAL,),
        in_specs=[
            pl.BlockSpec((1, C, D), lambda r: (r, 0, 0)),
            part(0),
            part(1),
            part(2),
            anywhere(),
        ],
        out_specs=[
            pl.BlockSpec((64, GROUPS, 8, HALF), lambda r: (0, 0, 0, 0)),
            pl.BlockSpec((16, HALF), lambda r: (0, 0)),
        ],
        out_shape=[like(64, GROUPS, 8, HALF), like(16, HALF)],
        scratch_shapes=[VMEM((ROWS_LOCAL, C, HALF), BF)],
    )(sig, w_qkv, w_qkv, w_qkv, after)


def columns_of(qkv, allowed, keep):
    for c in range(2):

        def store(lo, out):
            keep(c * 256 + lo, out)

        attend(qkv[c * 256 : (c + 1) * 256], allowed, store)


def own_kernel(meta, got_ref, w_qkv, by_x, out_ref, held, weight, sems):
    copies = [
        pltpu.make_async_copy(
            w_qkv.at[:, 256 * n + HALF : 256 * (n + 1)],
            weight.at[:, HALF * n : HALF * (n + 1)],
            sems.at[n],
        )
        for n in range(3)
    ]
    for copy in copies:
        copy.start()
    pick = one_hot(lambda o: (o % 64) * 2 + o // 64)
    for b in range(4):
        moved = move(pick, got_ref[b * BLOCK : (b + 1) * BLOCK, :])
        held[b * 64 : b * 64 + 64, :] = moved[:64]
        held[256 + b * 64 : 256 + b * 64 + 64, :] = moved[64:]
    core = core_of(meta)
    for n, d in enumerate((0,) + STEPS):
        for far, on in enumerate((core, 1 - core)):
            lo = (4 * far + n) * BLOCK
            source = pl.multiple_of((lax.rem(x_of(meta) + 4 - d, 4) * 2 + on) * BLOCK, BLOCK)
            by_x[:, lo : lo + BLOCK] = held[:, pl.ds(source, BLOCK)]

    def keep(lo, out):
        out_ref[lo : lo + BLOCK, :] = out

    for copy in copies:
        copy.wait()
    qkv = jnp.dot(held[...], weight[...], preferred_element_type=F32)
    columns_of(qkv, causal(), keep)


def own_part(meta, got, w_qkv):
    return call(
        own_kernel,
        "own_part",
        flops=10**12,
        moved=4 * MIB,
        vmem=20 * MIB,
        in_specs=[smem(), whole(), anywhere()],
        out_specs=[whole()] * 2,
        out_shape=[like(C, D), like(C, HALF)],
        scratch_shapes=[
            VMEM((C, D), BF),
            VMEM((D, 3 * HALF), BF),
            pltpu.SemaphoreType.DMA((3,)),
        ],
    )(meta, got, w_qkv)


def column_kernel(by_x, own, near, far, out_ref, near_v, far_v, outs, sems):
    copies = []
    for n in range(3):
        copies.append(pltpu.make_async_copy(near.at[n], near_v.at[n], sems.at[2 * n]))
        copies.append(pltpu.make_async_copy(far.at[n], far_v.at[n], sems.at[2 * n + 1]))
    for copy in copies:
        copy.start()
    allowed = causal()
    outs[:, :HALF] = own[...]
    half = 4 * BLOCK
    for n in range(3):

        def keep(lo, out):
            outs[lo : lo + BLOCK, (n + 1) * HALF : (n + 2) * HALF] = out

        copies[2 * n].wait()
        copies[2 * n + 1].wait()
        qkv = jnp.dot(
            by_x[:, :half], near_v[n].reshape(half, 3 * HALF), preferred_element_type=F32
        ) + jnp.dot(by_x[:, half:], far_v[n].reshape(half, 3 * HALF), preferred_element_type=F32)
        columns_of(qkv, allowed, keep)
    back = one_hot(lambda o: (o % 2) * 64 + o // 2)
    for b in range(4):
        both = jnp.concatenate(
            [outs[b * 64 : b * 64 + 64, :], outs[256 + b * 64 : 256 + b * 64 + 64, :]], axis=0
        )
        out_ref[b * BLOCK : (b + 1) * BLOCK, :] = move(back, both)


def column_part(by_x, own, near, far):
    return call(
        column_kernel,
        "column_part",
        flops=3 * 10**9,
        moved=6 * MIB,
        vmem=20 * MIB,
        in_specs=[whole()] * 2 + [anywhere()] * 2,
        out_specs=whole(),
        out_shape=like(C, C),
        scratch_shapes=[
            VMEM((3, 4, BLOCK, 3 * HALF), BF),
            VMEM((3, 4, BLOCK, 3 * HALF), BF),
            VMEM((C, C), BF),
            pltpu.SemaphoreType.DMA((6,)),
        ],
    )(by_x, own, near, far)


def mix_kernel(meta, columns, rows, w_out, near, far, out_ref):
    core = core_of(meta)
    y = y_of(meta)
    left = jnp.concatenate(
        [columns[...]]
        + [
            rows[:, lax.rem(group_of(meta) + GROUPS - k, GROUPS)].reshape(C, HALF)
            for k in (0,) + ORDER
        ],
        axis=1,
    )
    blocks = (
        (near, 0, y * 2 + core),
        (near, 1, (1 - y) * 2 + core),
        (far, 0, y * 2 + 1 - core),
        (far, 1, (1 - y) * 2 + 1 - core),
    )
    for source, n, j in blocks:
        own = w_out[:, pl.ds(pl.multiple_of(j * 256, 256), 256)]
        weight = jnp.concatenate(
            [
                own[HALF:],
                source[n, :, :, :256].reshape(3 * BLOCK, 256),
                own[:HALF],
                source[n, :, :, 256:].reshape(3 * BLOCK, 256),
            ],
            axis=0,
        )
        mixed = jnp.dot(left, weight, preferred_element_type=F32)
        out_ref[:, j] = mixed.astype(BF).reshape(64, 8, 256)


def mix(meta, columns, rows, w_out, near, far):
    return call(
        mix_kernel,
        "mix",
        flops=10**9,
        moved=6 * MIB,
        vmem=20 * MIB,
        in_specs=[smem()] + [whole()] * 5,
        out_specs=whole(),
        out_shape=like(64, GROUPS, 8, 256),
    )(meta, columns, rows, w_out, near, far)


def join_kernel(got_ref, out_ref):
    j = pl.program_id(0)
    pick = one_hot(lambda o: ((o // 2) % 16) * 8 + (o // 32) * 2 + o % 2)
    for b in range(4):
        moved = move(pick, got_ref[b * 16 : (b + 1) * 16, j].reshape(BLOCK, 256))
        for r in range(ROWS_LOCAL):
            out_ref[r, 0, b * 32 : (b + 1) * 32] = moved[r * 32 : (r + 1) * 32]


def join(got):
    return call(
        join_kernel,
        "join",
        flops=10**8,
        moved=4 * MIB,
        vmem=16 * MIB,
        grid=(GROUPS,),
        in_specs=[whole()],
        out_specs=pl.BlockSpec((ROWS_LOCAL, 1, BLOCK, 256), lambda j: (0, j, 0, 0)),
        out_shape=like(ROWS_LOCAL, GROUPS, BLOCK, 256),
    )(got)


def to_group(data, k):
    return lax.ppermute(data, "heads", [(j, (j + k) % GROUPS) for j in range(GROUPS)])


def along_x(data, d):
    return lax.ppermute(
        data, "rows", [(i, i // 8 * 8 + (i // 2 % 4 + d) % 4 * 2 + i % 2) for i in range(64)]
    )


def other_y(data):
    return lax.ppermute(data, "rows", [(i, i ^ 8) for i in range(64)])


def other_core(data):
    return lax.ppermute(data, "rows", [(i, i ^ 1) for i in range(64)])


def local(signal, w_qkv, w_out):
    meta = lax.axis_index(("rows", "heads")).astype(jnp.int32).reshape(1)
    sig = signal.reshape(ROWS_LOCAL, C, D)

    send = prep(meta, sig)
    own_rows, rows_done = row_part(sig, w_qkv, send)
    got = lax.all_to_all(
        send.reshape(64, 8, D), "rows", split_axis=0, concat_axis=0, tiled=True
    ).reshape(C, D)
    rows = lax.all_to_all(
        own_rows.reshape(64 * GROUPS, 8, HALF), BOTH, split_axis=0, concat_axis=0, tiled=True
    ).reshape(64, GROUPS, 8, HALF)

    mine = cut(meta, w_qkv, w_out)
    others, blocks = mid([to_group(mine, k) for k in ORDER], rows_done)
    near, blocks = stack(
        [others] + [along_x(others, d) for d in STEPS] + [blocks, other_y(blocks)], got
    )
    far = other_core(near)
    far_blocks = other_core(blocks)

    by_x, own = own_part(meta, got, w_qkv)
    columns = column_part(by_x, own, near, far)
    mixed = mix(meta, columns, rows, w_out, blocks, far_blocks).reshape(64 * GROUPS, 8, 256)
    back = lax.all_to_all(mixed, BOTH, split_axis=0, concat_axis=0, tiled=True)
    return join(back.reshape(64, GROUPS, 8, 256)).reshape(ROWS_LOCAL * C, 256)


def solution(mesh):
    return jax.shard_map(
        local,
        mesh=mesh,
        in_specs=(P("rows", None), P(None, "heads"), P("heads", None)),
        out_specs=P("rows", "heads"),
        check_vma=False,
    )
```

```python
import jax
import jax.numpy as jnp
from jax import lax
from jax.experimental import pallas as pl
from jax.experimental.pallas import tpu as pltpu
from jax.sharding import PartitionSpec as P

D = 1024
HEADS = 16
C = 512
GROUPS = 4
DIM = 64
HALF = 128
ROWS_LOCAL = 4
BLOCK = 128
BF = jnp.bfloat16
F32 = jnp.float32
VMEM = pltpu.VMEM
MIB = 1 << 20
ORDER = (2, 1, 3)
STEPS = (2, 3, 1)
WIDE = 5 * HALF
BOTH = ("heads", "rows")
SCALE = 0.125 * 1.4426950408889634


def whole():
    return pl.BlockSpec(memory_space=VMEM)


def anywhere():
    return pl.BlockSpec(memory_space=pl.ANY)


def smem():
    return pl.BlockSpec(memory_space=pltpu.SMEM)


def group_of(meta):
    return meta[0] & 3


def x_of(meta):
    return (meta[0] >> 3) & 3


def core_of(meta):
    return (meta[0] >> 2) & 1


def y_of(meta):
    return (meta[0] >> 5) & 1


def one_hot(source_of):
    out_at = lax.broadcasted_iota(jnp.int32, (BLOCK, BLOCK), 0)
    in_at = lax.broadcasted_iota(jnp.int32, (BLOCK, BLOCK), 1)
    return (in_at == source_of(out_at)).astype(F32).astype(BF)


def move(pick, data):
    return jnp.dot(pick, data, preferred_element_type=F32).astype(BF)


def causal():
    at_query = lax.broadcasted_iota(jnp.int32, (2 * BLOCK, BLOCK), 0) % BLOCK
    return lax.broadcasted_iota(jnp.int32, (2 * BLOCK, BLOCK), 1) <= at_query


def attend(qkv, allowed, store):
    length = qkv.shape[0]
    first = lax.broadcasted_iota(jnp.int32, (1, HALF), 1) < DIM
    query = qkv[:, :HALF]
    query_a = jnp.where(first, query, 0.0).astype(BF)
    query_b = jnp.where(first, 0.0, query).astype(BF)
    key = qkv[:, HALF : 2 * HALF].astype(BF)
    value = qkv[:, 2 * HALF :].astype(BF)
    value = jnp.concatenate([value, jnp.ones((length, HALF), BF)], axis=1)
    for block in range(length // BLOCK):
        lo = block * BLOCK
        hi = lo + BLOCK
        both = jnp.concatenate([query_a[lo:hi], query_b[lo:hi]], axis=0)
        scores = lax.dot_general(
            both, key[:hi], (((1,), (1,)), ((), ())), preferred_element_type=F32
        )
        pieces = [scores[:, n * BLOCK : (n + 1) * BLOCK] for n in range(block)]
        pieces.append(jnp.where(allowed, scores[:, lo:], F32(-1e30)))
        top = pieces[0]
        for piece in pieces[1:]:
            top = jnp.maximum(top, piece)
        top = jnp.max(top, axis=-1, keepdims=True)
        expo = [jnp.exp2((piece - top) * F32(SCALE)).astype(BF) for piece in pieces]
        out = jnp.dot(jnp.concatenate(expo, axis=1), value[:hi], preferred_element_type=F32)
        out = jnp.where(jnp.concatenate([first, first], axis=1), out[:BLOCK], out[BLOCK:])
        store(lo, (out[:, :HALF] / out[:, HALF:]).astype(BF))


def call(kernel, name, flops=0, moved=MIB, vmem=56 * MIB, **options):
    return pl.pallas_call(
        kernel,
        compiler_params=pltpu.CompilerParams(vmem_limit_bytes=vmem),
        cost_estimate=pl.CostEstimate(flops=flops, bytes_accessed=moved, transcendentals=0),
        name=name,
        **options,
    )


def like(*shape):
    return jax.ShapeDtypeStruct(shape, BF)


def cut_kernel(meta, query_ref, key_ref, value_ref, mix_ref, out_ref):
    out_ref[:, :HALF] = query_ref[...]
    out_ref[:, HALF : 2 * HALF] = key_ref[...]
    out_ref[:, 2 * HALF : 3 * HALF] = value_ref[...]
    out_ref[:, 3 * HALF : 5 * HALF] = mix_ref[HALF:, :]
    out_ref[:, 5 * HALF :] = mix_ref[:HALF, :]


def cut(meta, w_qkv, w_out):
    def part(n):
        return pl.BlockSpec((BLOCK, HALF), lambda b, meta: (x_of(meta) * 2 + core_of(meta), 2 * n + 1))

    return call(
        cut_kernel,
        "cut",
        grid_spec=pltpu.PrefetchScalarGridSpec(
            num_scalar_prefetch=1,
            grid=(1,),
            in_specs=[
                part(0),
                part(1),
                part(2),
                pl.BlockSpec((256, 256), lambda b, meta: (0, y_of(meta) * 2 + core_of(meta))),
            ],
            out_specs=pl.BlockSpec((BLOCK, 7 * HALF), lambda b, meta: (0, 0)),
        ),
        out_shape=like(BLOCK, 7 * HALF),
    )(meta, w_qkv, w_qkv, w_qkv, w_out)


def mid_kernel(in0, in1, in2, after, x_ref, y_ref):
    for n, ref in enumerate((in0, in1, in2)):
        x_ref[n] = ref[:, : 3 * HALF]
        y_ref[n] = ref[:, 3 * HALF :]


def mid(parts, after):
    return call(
        mid_kernel,
        "mid",
        flops=10**12,
        vmem=16 * MIB,
        in_specs=[whole()] * 3 + [anywhere()],
        out_specs=[whole()] * 2,
        out_shape=[like(3, BLOCK, 3 * HALF), like(3, BLOCK, 4 * HALF)],
    )(*parts, after)


def stack_kernel(in0, in1, in2, in3, block0, block1, after, out_ref, blocks_ref):
    for d, ref in enumerate((in0, in1, in2, in3)):
        for n in range(3):
            out_ref[n, d] = ref[n]
    blocks_ref[0] = block0[...]
    blocks_ref[1] = block1[...]


def stack(parts, after):
    return call(
        stack_kernel,
        "stack",
        flops=10**9,
        vmem=16 * MIB,
        in_specs=[whole()] * 6 + [anywhere()],
        out_specs=[whole()] * 2,
        out_shape=[like(3, 4, BLOCK, 3 * HALF), like(2, 3, BLOCK, 4 * HALF)],
    )(*parts, after)


def prep_kernel(meta, sig_ref, out_ref):
    pick = one_hot(lambda o: ((o // 2) % 4) * 32 + (o // 8) * 2 + o % 2)
    for b in range(2):
        part = sig_ref[:, b * 32 : (b + 1) * 32, :].reshape(BLOCK, D)
        out_ref[b * BLOCK : (b + 1) * BLOCK, :] = move(pick, part)


def prep(meta, sig):
    return call(
        prep_kernel,
        "prep",
        flops=2 * C * D * BLOCK,
        moved=2 * MIB,
        grid_spec=pltpu.PrefetchScalarGridSpec(
            num_scalar_prefetch=1,
            grid=(2,),
            in_specs=[pl.BlockSpec((4, 64, D), lambda b, meta: (0, group_of(meta) * 2 + b, 0))],
            out_specs=pl.BlockSpec((256, D), lambda b, meta: (b, 0)),
        ),
        out_shape=like(C, D),
    )(meta, sig)


def row_kernel(sig_ref, query_ref, key_ref, value_ref, after, out_ref, token_ref, held):
    r = pl.program_id(0)
    weight = jnp.concatenate([query_ref[...], key_ref[...], value_ref[...]], axis=1)
    qkv = jnp.dot(sig_ref[0], weight, preferred_element_type=F32)

    def store(lo, out):
        held[r, lo : lo + BLOCK, :] = out

    attend(qkv, causal(), store)

    @pl.when(r == ROWS_LOCAL - 1)
    def _():
        token_ref[...] = jnp.zeros_like(token_ref)
        pick = one_hot(lambda o: ((o // 2) % 4) * 32 + (o // 8) * 2 + o % 2)
        for j in range(GROUPS):
            for b in range(4):
                lo = j * BLOCK + b * 32
                part = held[:, lo : lo + 32, :].reshape(BLOCK, HALF)
                out_ref[j, b * 16 : (b + 1) * 16] = move(pick, part).reshape(16, 8, HALF)


def row_part(sig, w_qkv, after):
    def part(n):
        return pl.BlockSpec((D, HALF), lambda r: (0, 2 * n))

    return call(
        row_kernel,
        "row_part",
        moved=1,
        grid=(ROWS_LOCAL,),
        in_specs=[
            pl.BlockSpec((1, C, D), lambda r: (r, 0, 0)),
            part(0),
            part(1),
            part(2),
            anywhere(),
        ],
        out_specs=[
            pl.BlockSpec((GROUPS, 64, 8, HALF), lambda r: (0, 0, 0, 0)),
            pl.BlockSpec((16, HALF), lambda r: (0, 0)),
        ],
        out_shape=[like(GROUPS, 64, 8, HALF), like(16, HALF)],
        scratch_shapes=[VMEM((ROWS_LOCAL, C, HALF), BF)],
    )(sig, w_qkv, w_qkv, w_qkv, after)


def columns_of(qkv, allowed, keep):
    for c in range(2):

        def store(lo, out):
            keep(c * 256 + lo, out)

        attend(qkv[c * 256 : (c + 1) * 256], allowed, store)


def own_kernel(meta, got_ref, w_qkv, by_x, out_ref, held, weight, sems):
    copies = [
        pltpu.make_async_copy(
            w_qkv.at[:, 256 * n + HALF : 256 * (n + 1)],
            weight.at[:, HALF * n : HALF * (n + 1)],
            sems.at[n],
        )
        for n in range(3)
    ]
    for copy in copies:
        copy.start()
    pick = one_hot(lambda o: (o % 64) * 2 + o // 64)
    for b in range(4):
        moved = move(pick, got_ref[b * BLOCK : (b + 1) * BLOCK, :])
        held[b * 64 : b * 64 + 64, :] = moved[:64]
        held[256 + b * 64 : 256 + b * 64 + 64, :] = moved[64:]
    core = core_of(meta)
    for n, d in enumerate((0,) + STEPS):
        for far, on in enumerate((core, 1 - core)):
            lo = (4 * far + n) * BLOCK
            source = pl.multiple_of((lax.rem(x_of(meta) + 4 - d, 4) * 2 + on) * BLOCK, BLOCK)
            by_x[:, lo : lo + BLOCK] = held[:, pl.ds(source, BLOCK)]

    def keep(lo, out):
        out_ref[lo : lo + BLOCK, :] = out

    for copy in copies:
        copy.wait()
    qkv = jnp.dot(held[...], weight[...], preferred_element_type=F32)
    columns_of(qkv, causal(), keep)


def own_part(meta, got, w_qkv):
    return call(
        own_kernel,
        "own_part",
        flops=10**12,
        moved=4 * MIB,
        vmem=20 * MIB,
        in_specs=[smem(), whole(), anywhere()],
        out_specs=[whole()] * 2,
        out_shape=[like(C, D), like(C, HALF)],
        scratch_shapes=[
            VMEM((C, D), BF),
            VMEM((D, 3 * HALF), BF),
            pltpu.SemaphoreType.DMA((3,)),
        ],
    )(meta, got, w_qkv)


def column_kernel(by_x, own, near, far, out_ref, near_v, far_v, outs, sems):
    copies = []
    for n in range(3):
        copies.append(pltpu.make_async_copy(near.at[n], near_v.at[n], sems.at[2 * n]))
        copies.append(pltpu.make_async_copy(far.at[n], far_v.at[n], sems.at[2 * n + 1]))
    for copy in copies:
        copy.start()
    allowed = causal()
    outs[:, :HALF] = own[...]
    half = 4 * BLOCK
    for n in range(3):

        def keep(lo, out):
            outs[lo : lo + BLOCK, (n + 1) * HALF : (n + 2) * HALF] = out

        copies[2 * n].wait()
        copies[2 * n + 1].wait()
        qkv = jnp.dot(
            by_x[:, :half], near_v[n].reshape(half, 3 * HALF), preferred_element_type=F32
        ) + jnp.dot(by_x[:, half:], far_v[n].reshape(half, 3 * HALF), preferred_element_type=F32)
        columns_of(qkv, allowed, keep)
    back = one_hot(lambda o: (o % 2) * 64 + o // 2)
    for b in range(4):
        both = jnp.concatenate(
            [outs[b * 64 : b * 64 + 64, :], outs[256 + b * 64 : 256 + b * 64 + 64, :]], axis=0
        )
        out_ref[b * BLOCK : (b + 1) * BLOCK, :] = move(back, both)


def column_part(by_x, own, near, far):
    return call(
        column_kernel,
        "column_part",
        flops=3 * 10**9,
        moved=6 * MIB,
        vmem=20 * MIB,
        in_specs=[whole()] * 2 + [anywhere()] * 2,
        out_specs=whole(),
        out_shape=like(C, C),
        scratch_shapes=[
            VMEM((3, 4, BLOCK, 3 * HALF), BF),
            VMEM((3, 4, BLOCK, 3 * HALF), BF),
            VMEM((C, C), BF),
            pltpu.SemaphoreType.DMA((6,)),
        ],
    )(by_x, own, near, far)


def mix_kernel(meta, columns, rows, w_out, near, far, out_ref):
    core = core_of(meta)
    y = y_of(meta)
    left = jnp.concatenate(
        [columns[...]]
        + [
            rows[lax.rem(group_of(meta) + GROUPS - k, GROUPS)].reshape(C, HALF)
            for k in (0,) + ORDER
        ],
        axis=1,
    )
    blocks = (
        (near, 0, y * 2 + core),
        (near, 1, (1 - y) * 2 + core),
        (far, 0, y * 2 + 1 - core),
        (far, 1, (1 - y) * 2 + 1 - core),
    )
    for source, n, j in blocks:
        own = w_out[:, pl.ds(pl.multiple_of(j * 256, 256), 256)]
        weight = jnp.concatenate(
            [
                own[HALF:],
                source[n, :, :, :256].reshape(3 * BLOCK, 256),
                own[:HALF],
                source[n, :, :, 256:].reshape(3 * BLOCK, 256),
            ],
            axis=0,
        )
        mixed = jnp.dot(left, weight, preferred_element_type=F32)
        out_ref[j] = mixed.astype(BF).reshape(64, 8, 256)


def mix(meta, columns, rows, w_out, near, far):
    return call(
        mix_kernel,
        "mix",
        flops=10**9,
        moved=6 * MIB,
        vmem=20 * MIB,
        in_specs=[smem()] + [whole()] * 5,
        out_specs=whole(),
        out_shape=like(GROUPS, 64, 8, 256),
    )(meta, columns, rows, w_out, near, far)


def join_kernel(got_ref, out_ref):
    j = pl.program_id(0)
    pick = one_hot(lambda o: ((o // 2) % 16) * 8 + (o // 32) * 2 + o % 2)
    for b in range(4):
        moved = move(pick, got_ref[j, b * 16 : (b + 1) * 16].reshape(BLOCK, 256))
        for r in range(ROWS_LOCAL):
            out_ref[r, 0, b * 32 : (b + 1) * 32] = moved[r * 32 : (r + 1) * 32]


def join(got):
    return call(
        join_kernel,
        "join",
        flops=10**8,
        moved=4 * MIB,
        vmem=16 * MIB,
        grid=(GROUPS,),
        in_specs=[whole()],
        out_specs=pl.BlockSpec((ROWS_LOCAL, 1, BLOCK, 256), lambda j: (0, j, 0, 0)),
        out_shape=like(ROWS_LOCAL, GROUPS, BLOCK, 256),
    )(got)


def to_group(data, k):
    return lax.ppermute(data, "heads", [(j, (j + k) % GROUPS) for j in range(GROUPS)])


def along_x(data, d):
    return lax.ppermute(
        data, "rows", [(i, i // 8 * 8 + (i // 2 % 4 + d) % 4 * 2 + i % 2) for i in range(64)]
    )


def other_y(data):
    return lax.ppermute(data, "rows", [(i, i ^ 8) for i in range(64)])


def other_core(data):
    return lax.ppermute(data, "rows", [(i, i ^ 1) for i in range(64)])


def local(signal, w_qkv, w_out):
    meta = lax.axis_index(("rows", "heads")).astype(jnp.int32).reshape(1)
    sig = signal.reshape(ROWS_LOCAL, C, D)

    send = prep(meta, sig)
    own_rows, rows_done = row_part(sig, w_qkv, send)
    got = lax.all_to_all(
        send.reshape(64, 8, D), "rows", split_axis=0, concat_axis=0, tiled=True
    ).reshape(C, D)
    rows = lax.all_to_all(
        own_rows.reshape(64 * GROUPS, 8, HALF), BOTH, split_axis=0, concat_axis=0, tiled=True
    ).reshape(GROUPS, 64, 8, HALF)

    mine = cut(meta, w_qkv, w_out)
    others, blocks = mid([to_group(mine, k) for k in ORDER], rows_done)
    near, blocks = stack(
        [others] + [along_x(others, d) for d in STEPS] + [blocks, other_y(blocks)], got
    )
    far = other_core(near)
    far_blocks = other_core(blocks)

    by_x, own = own_part(meta, got, w_qkv)
    columns = column_part(by_x, own, near, far)
    mixed = mix(meta, columns, rows, w_out, blocks, far_blocks).reshape(64 * GROUPS, 8, 256)
    back = lax.all_to_all(mixed, BOTH, split_axis=0, concat_axis=0, tiled=True)
    return join(back.reshape(GROUPS, 64, 8, 256)).reshape(ROWS_LOCAL * C, 256)


def solution(mesh):
    return jax.shard_map(
        local,
        mesh=mesh,
        in_specs=(P("rows", None), P(None, "heads"), P("heads", None)),
        out_specs=P("rows", "heads"),
        check_vma=False,
    )
```

```python
import jax
import jax.numpy as jnp
from jax import lax
from jax.experimental import pallas as pl
from jax.experimental.pallas import tpu as pltpu
from jax.sharding import PartitionSpec as P

D = 1024
HEADS = 16
C = 512
GROUPS = 4
DIM = 64
HALF = 128
ROWS_LOCAL = 4
BLOCK = 128
BF = jnp.bfloat16
F32 = jnp.float32
VMEM = pltpu.VMEM
MIB = 1 << 20
ORDER = (2, 1, 3)
STEPS = (2, 3, 1)
WIDE = 5 * HALF
BOTH = ("heads", "rows")
SCALE = 0.125 * 1.4426950408889634


def whole():
    return pl.BlockSpec(memory_space=VMEM)


def anywhere():
    return pl.BlockSpec(memory_space=pl.ANY)


def smem():
    return pl.BlockSpec(memory_space=pltpu.SMEM)


def group_of(meta):
    return meta[0] & 3


def x_of(meta):
    return (meta[0] >> 3) & 3


def core_of(meta):
    return (meta[0] >> 2) & 1


def y_of(meta):
    return (meta[0] >> 5) & 1


def one_hot(source_of):
    out_at = lax.broadcasted_iota(jnp.int32, (BLOCK, BLOCK), 0)
    in_at = lax.broadcasted_iota(jnp.int32, (BLOCK, BLOCK), 1)
    return (in_at == source_of(out_at)).astype(F32).astype(BF)


def move(pick, data):
    return jnp.dot(pick, data, preferred_element_type=F32).astype(BF)


def causal():
    at_query = lax.broadcasted_iota(jnp.int32, (2 * BLOCK, BLOCK), 0) % BLOCK
    return lax.broadcasted_iota(jnp.int32, (2 * BLOCK, BLOCK), 1) <= at_query


def attend(qkv, allowed, store):
    length = qkv.shape[0]
    first = lax.broadcasted_iota(jnp.int32, (1, HALF), 1) < DIM
    query = qkv[:, :HALF]
    query_a = jnp.where(first, query, 0.0).astype(BF)
    query_b = jnp.where(first, 0.0, query).astype(BF)
    key = qkv[:, HALF : 2 * HALF].astype(BF)
    value = qkv[:, 2 * HALF :].astype(BF)
    value = jnp.concatenate([value, jnp.ones((length, HALF), BF)], axis=1)
    for block in range(length // BLOCK):
        lo = block * BLOCK
        hi = lo + BLOCK
        both = jnp.concatenate([query_a[lo:hi], query_b[lo:hi]], axis=0)
        scores = lax.dot_general(
            both, key[:hi], (((1,), (1,)), ((), ())), preferred_element_type=F32
        )
        pieces = [scores[:, n * BLOCK : (n + 1) * BLOCK] for n in range(block)]
        pieces.append(jnp.where(allowed, scores[:, lo:], F32(-1e30)))
        top = pieces[0]
        for piece in pieces[1:]:
            top = jnp.maximum(top, piece)
        top = jnp.max(top, axis=-1, keepdims=True)
        expo = [jnp.exp2((piece - top) * F32(SCALE)).astype(BF) for piece in pieces]
        out = jnp.dot(jnp.concatenate(expo, axis=1), value[:hi], preferred_element_type=F32)
        out = jnp.where(jnp.concatenate([first, first], axis=1), out[:BLOCK], out[BLOCK:])
        store(lo, (out[:, :HALF] / out[:, HALF:]).astype(BF))


def call(kernel, name, flops=0, moved=MIB, vmem=56 * MIB, **options):
    return pl.pallas_call(
        kernel,
        compiler_params=pltpu.CompilerParams(vmem_limit_bytes=vmem),
        cost_estimate=pl.CostEstimate(flops=flops, bytes_accessed=moved, transcendentals=0),
        name=name,
        **options,
    )


def like(*shape):
    return jax.ShapeDtypeStruct(shape, BF)


def cut_kernel(meta, query_ref, key_ref, value_ref, mix_ref, out_ref):
    out_ref[:, :HALF] = query_ref[...]
    out_ref[:, HALF : 2 * HALF] = key_ref[...]
    out_ref[:, 2 * HALF : 3 * HALF] = value_ref[...]
    out_ref[:, 3 * HALF : 5 * HALF] = mix_ref[HALF:, :]
    out_ref[:, 5 * HALF :] = mix_ref[:HALF, :]


def cut(meta, w_qkv, w_out):
    def part(n):
        return pl.BlockSpec((BLOCK, HALF), lambda b, meta: (x_of(meta) * 2 + core_of(meta), 2 * n + 1))

    return call(
        cut_kernel,
        "cut",
        grid_spec=pltpu.PrefetchScalarGridSpec(
            num_scalar_prefetch=1,
            grid=(1,),
            in_specs=[
                part(0),
                part(1),
                part(2),
                pl.BlockSpec((256, 256), lambda b, meta: (0, y_of(meta) * 2 + core_of(meta))),
            ],
            out_specs=pl.BlockSpec((BLOCK, 7 * HALF), lambda b, meta: (0, 0)),
        ),
        out_shape=like(BLOCK, 7 * HALF),
    )(meta, w_qkv, w_qkv, w_qkv, w_out)


def mid_kernel(in0, in1, in2, after, x_ref, y_ref):
    for n, ref in enumerate((in0, in1, in2)):
        x_ref[n] = ref[:, : 3 * HALF]
        y_ref[n] = ref[:, 3 * HALF :]


def mid(parts, after):
    return call(
        mid_kernel,
        "mid",
        flops=10**12,
        vmem=16 * MIB,
        in_specs=[whole()] * 3 + [anywhere()],
        out_specs=[whole()] * 2,
        out_shape=[like(3, BLOCK, 3 * HALF), like(3, BLOCK, 4 * HALF)],
    )(*parts, after)


def stack_kernel(in0, in1, in2, in3, block0, block1, after, out_ref, blocks_ref):
    for d, ref in enumerate((in0, in1, in2, in3)):
        for n in range(3):
            out_ref[n, d] = ref[n]
    blocks_ref[0] = block0[...]
    blocks_ref[1] = block1[...]


def stack(parts, after):
    return call(
        stack_kernel,
        "stack",
        flops=10**9,
        vmem=16 * MIB,
        in_specs=[whole()] * 6 + [anywhere()],
        out_specs=[whole()] * 2,
        out_shape=[like(3, 4, BLOCK, 3 * HALF), like(2, 3, BLOCK, 4 * HALF)],
    )(*parts, after)


def prep_kernel(meta, sig_ref, out_ref):
    pick = one_hot(lambda o: ((o // 2) % 4) * 32 + (o // 8) * 2 + o % 2)
    for b in range(2):
        part = sig_ref[:, b * 32 : (b + 1) * 32, :].reshape(BLOCK, D)
        out_ref[b * BLOCK : (b + 1) * BLOCK, :] = move(pick, part)


def prep(meta, sig):
    return call(
        prep_kernel,
        "prep",
        flops=2 * C * D * BLOCK,
        moved=2 * MIB,
        grid_spec=pltpu.PrefetchScalarGridSpec(
            num_scalar_prefetch=1,
            grid=(2,),
            in_specs=[pl.BlockSpec((4, 64, D), lambda b, meta: (0, group_of(meta) * 2 + b, 0))],
            out_specs=pl.BlockSpec((256, D), lambda b, meta: (b, 0)),
        ),
        out_shape=like(C, D),
    )(meta, sig)


def row_kernel(sig_ref, query_ref, key_ref, value_ref, after, out_ref, token_ref, held):
    r = pl.program_id(0)
    weight = jnp.concatenate([query_ref[...], key_ref[...], value_ref[...]], axis=1)
    qkv = jnp.dot(sig_ref[0], weight, preferred_element_type=F32)

    def store(lo, out):
        held[r, lo : lo + BLOCK, :] = out

    attend(qkv, causal(), store)

    @pl.when(r == ROWS_LOCAL - 1)
    def _():
        token_ref[...] = jnp.zeros_like(token_ref)
        pick = one_hot(lambda o: ((o // 2) % 4) * 32 + (o // 8) * 2 + o % 2)
        for j in range(GROUPS):
            for b in range(4):
                lo = j * BLOCK + b * 32
                part = held[:, lo : lo + 32, :].reshape(BLOCK, HALF)
                out_ref[j, b * 16 : (b + 1) * 16] = move(pick, part).reshape(16, 8, HALF)


def row_part(sig, w_qkv, after):
    def part(n):
        return pl.BlockSpec((D, HALF), lambda r: (0, 2 * n))

    return call(
        row_kernel,
        "row_part",
        moved=1,
        grid=(ROWS_LOCAL,),
        in_specs=[
            pl.BlockSpec((1, C, D), lambda r: (r, 0, 0)),
            part(0),
            part(1),
            part(2),
            anywhere(),
        ],
        out_specs=[
            pl.BlockSpec((GROUPS, 64, 8, HALF), lambda r: (0, 0, 0, 0)),
            pl.BlockSpec((16, HALF), lambda r: (0, 0)),
        ],
        out_shape=[like(GROUPS, 64, 8, HALF), like(16, HALF)],
        scratch_shapes=[VMEM((ROWS_LOCAL, C, HALF), BF)],
    )(sig, w_qkv, w_qkv, w_qkv, after)


def columns_of(qkv, allowed, keep):
    for c in range(2):

        def store(lo, out):
            keep(c * 256 + lo, out)

        attend(qkv[c * 256 : (c + 1) * 256], allowed, store)


def own_kernel(meta, got_ref, w_qkv, by_x, out_ref, held, weight, sems):
    copies = [
        pltpu.make_async_copy(
            w_qkv.at[:, 256 * n + HALF : 256 * (n + 1)],
            weight.at[:, HALF * n : HALF * (n + 1)],
            sems.at[n],
        )
        for n in range(3)
    ]
    for copy in copies:
        copy.start()
    pick = one_hot(lambda o: (o % 64) * 2 + o // 64)
    for b in range(4):
        moved = move(pick, got_ref[b * BLOCK : (b + 1) * BLOCK, :])
        held[b * 64 : b * 64 + 64, :] = moved[:64]
        held[256 + b * 64 : 256 + b * 64 + 64, :] = moved[64:]
    core = core_of(meta)
    for n, d in enumerate((0,) + STEPS):
        for far, on in enumerate((core, 1 - core)):
            lo = (4 * far + n) * BLOCK
            source = pl.multiple_of((lax.rem(x_of(meta) + 4 - d, 4) * 2 + on) * BLOCK, BLOCK)
            by_x[:, lo : lo + BLOCK] = held[:, pl.ds(source, BLOCK)]

    def keep(lo, out):
        out_ref[lo : lo + BLOCK, :] = out

    for copy in copies:
        copy.wait()
    qkv = jnp.dot(held[...], weight[...], preferred_element_type=F32)
    columns_of(qkv, causal(), keep)


def own_part(meta, got, w_qkv):
    return call(
        own_kernel,
        "own_part",
        flops=10**12,
        moved=4 * MIB,
        vmem=20 * MIB,
        in_specs=[smem(), whole(), anywhere()],
        out_specs=[whole()] * 2,
        out_shape=[like(C, D), like(C, HALF)],
        scratch_shapes=[
            VMEM((C, D), BF),
            VMEM((D, 3 * HALF), BF),
            pltpu.SemaphoreType.DMA((3,)),
        ],
    )(meta, got, w_qkv)


def column_kernel(by_x, own, near, far, out_ref, near_v, far_v, outs, sems):
    copies = []
    for n in range(3):
        copies.append(pltpu.make_async_copy(near.at[n], near_v.at[n], sems.at[2 * n]))
        copies.append(pltpu.make_async_copy(far.at[n], far_v.at[n], sems.at[2 * n + 1]))
    for copy in copies:
        copy.start()
    allowed = causal()
    outs[:, :HALF] = own[...]
    half = 4 * BLOCK
    for n in range(3):

        def keep(lo, out):
            outs[lo : lo + BLOCK, (n + 1) * HALF : (n + 2) * HALF] = out

        copies[2 * n].wait()
        copies[2 * n + 1].wait()
        qkv = jnp.dot(
            by_x[:, :half], near_v[n].reshape(half, 3 * HALF), preferred_element_type=F32
        ) + jnp.dot(by_x[:, half:], far_v[n].reshape(half, 3 * HALF), preferred_element_type=F32)
        columns_of(qkv, allowed, keep)
    back = one_hot(lambda o: (o % 2) * 64 + o // 2)
    for b in range(4):
        both = jnp.concatenate(
            [outs[b * 64 : b * 64 + 64, :], outs[256 + b * 64 : 256 + b * 64 + 64, :]], axis=0
        )
        out_ref[b * BLOCK : (b + 1) * BLOCK, :] = move(back, both)


def column_part(by_x, own, near, far):
    return call(
        column_kernel,
        "column_part",
        flops=3 * 10**9,
        moved=6 * MIB,
        vmem=20 * MIB,
        in_specs=[whole()] * 2 + [anywhere()] * 2,
        out_specs=whole(),
        out_shape=like(C, C),
        scratch_shapes=[
            VMEM((3, 4, BLOCK, 3 * HALF), BF),
            VMEM((3, 4, BLOCK, 3 * HALF), BF),
            VMEM((C, C), BF),
            pltpu.SemaphoreType.DMA((6,)),
        ],
    )(by_x, own, near, far)


def mix_kernel(meta, columns, rows, w_out, near, far, out_ref):
    core = core_of(meta)
    y = y_of(meta)
    left = jnp.concatenate(
        [columns[...]]
        + [
            rows[lax.rem(group_of(meta) + GROUPS - k, GROUPS)].reshape(C, HALF)
            for k in (0,) + ORDER
        ],
        axis=1,
    )
    blocks = (
        (near, 0, y * 2 + core),
        (near, 1, (1 - y) * 2 + core),
        (far, 0, y * 2 + 1 - core),
        (far, 1, (1 - y) * 2 + 1 - core),
    )
    for source, n, j in blocks:
        own = w_out[:, pl.ds(pl.multiple_of(j * 256, 256), 256)]
        weight = jnp.concatenate(
            [
                own[HALF:],
                source[n, :, :, :256].reshape(3 * BLOCK, 256),
                own[:HALF],
                source[n, :, :, 256:].reshape(3 * BLOCK, 256),
            ],
            axis=0,
        )
        mixed = jnp.dot(left, weight, preferred_element_type=F32)
        out_ref[j] = mixed.astype(BF).reshape(64, 8, 256)


def mix(meta, columns, rows, w_out, near, far):
    return call(
        mix_kernel,
        "mix",
        flops=10**9,
        moved=6 * MIB,
        vmem=20 * MIB,
        in_specs=[smem()] + [whole()] * 5,
        out_specs=whole(),
        out_shape=like(GROUPS, 64, 8, 256),
    )(meta, columns, rows, w_out, near, far)


def join_kernel(got_ref, out_ref):
    pick = one_hot(lambda o: ((o // 2) % 16) * 8 + (o // 32) * 2 + o % 2)
    for n in range(2):
        j = pl.program_id(0) * 2 + n
        for b in range(4):
            moved = move(pick, got_ref[j, b * 16 : (b + 1) * 16].reshape(BLOCK, 256))
            for r in range(ROWS_LOCAL):
                out_ref[r, n, b * 32 : (b + 1) * 32] = moved[r * 32 : (r + 1) * 32]


def join(got):
    return call(
        join_kernel,
        "join",
        flops=10**8,
        moved=4 * MIB,
        vmem=16 * MIB,
        grid=(2,),
        in_specs=[whole()],
        out_specs=pl.BlockSpec((ROWS_LOCAL, 2, BLOCK, 256), lambda j: (0, j, 0, 0)),
        out_shape=like(ROWS_LOCAL, GROUPS, BLOCK, 256),
    )(got)


def to_group(data, k):
    return lax.ppermute(data, "heads", [(j, (j + k) % GROUPS) for j in range(GROUPS)])


def along_x(data, d):
    return lax.ppermute(
        data, "rows", [(i, i // 8 * 8 + (i // 2 % 4 + d) % 4 * 2 + i % 2) for i in range(64)]
    )


def other_y(data):
    return lax.ppermute(data, "rows", [(i, i ^ 8) for i in range(64)])


def other_core(data):
    return lax.ppermute(data, "rows", [(i, i ^ 1) for i in range(64)])


def local(signal, w_qkv, w_out):
    meta = lax.axis_index(("rows", "heads")).astype(jnp.int32).reshape(1)
    sig = signal.reshape(ROWS_LOCAL, C, D)

    send = prep(meta, sig)
    own_rows, rows_done = row_part(sig, w_qkv, send)
    got = lax.all_to_all(
        send.reshape(64, 8, D), "rows", split_axis=0, concat_axis=0, tiled=True
    ).reshape(C, D)
    rows = lax.all_to_all(
        own_rows.reshape(64 * GROUPS, 8, HALF), BOTH, split_axis=0, concat_axis=0, tiled=True
    ).reshape(GROUPS, 64, 8, HALF)

    mine = cut(meta, w_qkv, w_out)
    others, blocks = mid([to_group(mine, k) for k in ORDER], rows_done)
    near, blocks = stack(
        [others] + [along_x(others, d) for d in STEPS] + [blocks, other_y(blocks)], got
    )
    far = other_core(near)
    far_blocks = other_core(blocks)

    by_x, own = own_part(meta, got, w_qkv)
    columns = column_part(by_x, own, near, far)
    mixed = mix(meta, columns, rows, w_out, blocks, far_blocks).reshape(64 * GROUPS, 8, 256)
    back = lax.all_to_all(mixed, BOTH, split_axis=0, concat_axis=0, tiled=True)
    return join(back.reshape(GROUPS, 64, 8, 256)).reshape(ROWS_LOCAL * C, 256)


def solution(mesh):
    return jax.shard_map(
        local,
        mesh=mesh,
        in_specs=(P("rows", None), P(None, "heads"), P("heads", None)),
        out_specs=P("rows", "heads"),
        check_vma=False,
    )
```
